256 devices in a mesh: row: 8 (over x, core), col: 32 (over z, y).
Axes of the slice: x: 4, y: 4, z: 8, core: 2. Of those that a mesh axis runs over, the one named last changes fastest.
Arguments:
- embeddings: bfloat16 [256, 131072], P(None, ('row', 'col')), may hold values from -10.1875 to 10.1875
- vectors: float32 [32, 131072], P(None, ('row', 'col')), may hold values from -17 to 17
- block_pairs: int32 [6144, 2], P(('row', 'col')), may hold values from 0 to 255, as said below
- counts: int32 [256], P(('row', 'col')), may hold values from 1 to 24, as said below
Outputs:
- embedding_basis: float32 [32, 131072], P(None, ('row', 'col'))
- gram_factor: float32 [32, 32], replicated
The draws below stay inside these ranges and needn't reach their ends.
Inputs may be any that keep to these rules, and one draw needn't show every extreme that they name: `block_pairs`: device d = r * 32 + c of row+col lists in its first counts[d] rows only pairs (I, J) with I <= J, I // 32 == r and J % 32 == c; its first row is (d, d); each pair appears at most once among the listed rows of all devices. Its other rows hold block numbers and are ignored. `counts`: the most, 24, is reached in every draw.
All inputs are finite; a program needn't handle non-finite values.
Results may differ from the reference program's by a relative error of at most 0.004.
Values may be sent and summed in bfloat16 or wider, within the bound.
No kernel may reach another device: no remote copies, remote signals or barrier semaphores. Data moves between devices by JAX's collectives and lax.ppermute only.
A program may use at most 256 MiB of HBM per device.

```python
import math
import jax
import jax.numpy as jnp
from jax import lax

BS = 512
EMB = 256
VEC = 32
MAXP = 24
NPTS = 131072
N_ROW = 8
N_COL = 32


def listing(key):
    row_devices = N_ROW
    col_devices = N_COL
    slot_total = row_devices * col_devices
    key_wanted, key_shuffle = jax.random.split(key)
    wanted = jax.random.randint(key_wanted, (slot_total,), max(1, MAXP // 4), MAXP + 1)
    device = jnp.arange(slot_total, dtype=jnp.int32)
    row_index = device // col_devices
    col_index = device % col_devices
    candidate = jnp.arange(slot_total, dtype=jnp.int32)
    near_slot = candidate // row_devices
    far_slot = candidate % row_devices
    row_block = row_index[:, None] * col_devices + near_slot[None, :]
    col_block = far_slot[None, :] * col_devices + col_index[:, None]
    usable_mask = (row_block <= col_block).astype(jnp.int32)
    diagonal = (row_block == col_block).astype(jnp.int32)
    shuffle = jax.vmap(lambda single: jax.random.permutation(single, slot_total))(jax.random.split(key_shuffle, slot_total))
    ranking = usable_mask * (2 * slot_total) + diagonal * slot_total + shuffle.astype(jnp.int32)
    picked = jnp.argsort(-ranking, axis=1, stable=True)[:, :MAXP]
    usable = jnp.sum(usable_mask, axis=1)
    listed = jnp.minimum(usable, wanted)
    listed = jnp.where(device == col_devices - 1, MAXP, listed)
    chosen_rows = jnp.take_along_axis(row_block, picked, axis=1)
    chosen_cols = jnp.take_along_axis(col_block, picked, axis=1)
    stacked = jnp.stack([chosen_rows, chosen_cols], axis=-1).reshape(slot_total * MAXP, 2)
    return (stacked.astype(jnp.int32), listed.astype(jnp.int32))


def draw_block_pairs(key, part):
    shared = listing(key)[0]
    return shared


def draw_counts(key, part):
    shared = listing(key)[1]
    return shared


def draw_vectors(key, part):
    key = jax.random.fold_in(key, 7)
    key_main = jax.random.fold_in(key, 0)
    values = jnp.clip(jax.random.normal(key_main, (VEC, NPTS)), -6.0, 6.0)
    return values.astype(jnp.float32)


def shard_levels(own_key, extent, cuts, least, top_value):
    level, own = 1.0, jax.random.fold_in(own_key, 6)
    for position, parts in cuts:
        draws = jnp.exp(jax.random.uniform(jax.random.fold_in(own, position), (parts,), jnp.float32, least / len(cuts), top_value / len(cuts)))
        level = level * jnp.repeat(draws, extent[position] // parts).reshape([-1 if axis == position else 1 for axis in range(len(extent))])
    return level


def centred(key, extent, scale, most, shards=(), kind=jnp.bfloat16):
    level = shard_levels(key, extent, shards, -0.22, 0.18) if shards else 1.0
    entries = jax.random.normal(key, extent, jnp.float32) * scale * level
    return jnp.minimum(jnp.maximum(entries, -most), most).astype(kind)


def setup_inputs(seed: int = 0) -> dict:
    arg_keys = jax.random.split(jax.random.key(seed), 5)
    return {
        "embeddings": centred(arg_keys[0], (EMB, NPTS), 1.7, 10.1875, ((1, 256),)),
        "vectors": draw_vectors(jax.random.fold_in(arg_keys[4], 71), 0),
        "block_pairs": draw_block_pairs(jax.random.fold_in(arg_keys[4], 71), 0),
        "counts": draw_counts(jax.random.fold_in(arg_keys[4], 71), 0),
    }


def reference(embeddings, vectors, block_pairs, counts):
    vector_bf16 = vectors.astype(jnp.bfloat16)
    score_scale = 1.0 / math.sqrt(EMB)

    def add_tile(totals, slot_number):
        image_sum, degree = totals
        row_block = block_pairs[slot_number, 0]
        col_block = block_pairs[slot_number, 1]
        row_start = (row_block * BS).astype(jnp.int32)
        col_start = (col_block * BS).astype(jnp.int32)
        near_embed = lax.dynamic_slice_in_dim(embeddings, row_start, BS, 1)
        far_embed = lax.dynamic_slice_in_dim(embeddings, col_start, BS, 1)
        scores = jnp.dot(near_embed.T.astype(jnp.float32), far_embed.astype(jnp.float32), preferred_element_type=jnp.float32)
        weights = jax.nn.sigmoid(scores * score_scale)
        tile_bf16 = weights.astype(jnp.bfloat16)
        mirror_mask = (row_block != col_block).astype(jnp.float32)
        near_vec = lax.dynamic_slice_in_dim(vector_bf16, row_start, BS, 1)
        far_vec = lax.dynamic_slice_in_dim(vector_bf16, col_start, BS, 1)
        near_terms = jnp.dot(far_vec.astype(jnp.float32), tile_bf16.T.astype(jnp.float32), preferred_element_type=jnp.float32)
        far_terms = jnp.dot(near_vec.astype(jnp.float32), tile_bf16.astype(jnp.float32), preferred_element_type=jnp.float32) * mirror_mask
        row_mass = lax.optimization_barrier(jnp.sum(weights, axis=1))
        col_mass = lax.optimization_barrier(jnp.sum(weights, axis=0)) * mirror_mask
        current = lax.dynamic_slice_in_dim(image_sum, row_start, BS, 1)
        image_sum = lax.dynamic_update_slice_in_dim(image_sum, current + near_terms, row_start, 1)
        current = lax.dynamic_slice_in_dim(image_sum, col_start, BS, 1)
        image_sum = lax.dynamic_update_slice_in_dim(image_sum, current + far_terms, col_start, 1)
        current = lax.dynamic_slice_in_dim(degree, row_start, BS, 0)
        degree = lax.dynamic_update_slice_in_dim(degree, current + row_mass, row_start, 0)
        current = lax.dynamic_slice_in_dim(degree, col_start, BS, 0)
        degree = lax.dynamic_update_slice_in_dim(degree, current + col_mass, col_start, 0)
        return (image_sum, degree)

    def scan_slot(totals, slot_number):
        is_live = slot_number % MAXP < counts[slot_number // MAXP]
        totals = lax.cond(is_live, lambda current: add_tile(current, slot_number), lambda current: current, totals)
        return (totals, None)
    initial = (jnp.zeros((VEC, NPTS), jnp.float32), jnp.zeros((NPTS,), jnp.float32))
    (image_sum, degree), unused = lax.scan(scan_slot, initial, jnp.arange(block_pairs.shape[0], dtype=jnp.int32))
    walked = image_sum / degree[None, :]
    gram_matrix = jnp.dot(walked.astype(jnp.float32), walked.T.astype(jnp.float32), precision=lax.Precision.HIGHEST, preferred_element_type=jnp.float32) / NPTS
    gram_factor = jnp.linalg.cholesky(gram_matrix)
    inverse = lax.linalg.triangular_solve(gram_factor, jnp.eye(VEC, dtype=jnp.float32), left_side=True, lower=True)
    embedding_basis = jnp.dot(inverse.astype(jnp.float32), walked.astype(jnp.float32), precision=lax.Precision.HIGHEST, preferred_element_type=jnp.float32)
    return (embedding_basis, gram_factor)
```

```python
import functools
import math

import jax
import jax.numpy as jnp
from jax import lax
from jax.experimental import pallas as pl
from jax.experimental.pallas import tpu as pltpu
from jax.sharding import Mesh
from jax.sharding import PartitionSpec as P

X, K, Z, Y = 4, 2, 8, 4
COLS = Z * Y
NEAR = ("k", "z")
FAR = ("x", "y")
EVERY = ("x", "k", "z", "y")
WAYS = 16
BS = 512
EMB = 256
VEC = 32
AUG = 48
MAXP = 24
LISTS = K * Y
SLOTS = 256


def select_kernel(place_ref, lists_ref, picked_ref):
    own_y = place_ref[0]
    own_k = place_ref[1]

    def each_list(which, found):
        def each_slot(slot, found):
            row_block = lists_ref[which, 2 * slot]
            col_block = lists_ref[which, 2 * slot + 1]
            near = ((row_block >> 5) & 1) * Z + ((row_block >> 2) & 7)
            far = ((col_block >> 6) & 3) * Y + (col_block & 3)
            same = (row_block == col_block).astype(jnp.int32)
            mine = ((row_block & 3) == own_y) & (((col_block >> 5) & 1) == own_k)
            picked_ref[found + 1] = same * 256 + near * 16 + far
            return found + mine.astype(jnp.int32)

        return lax.fori_loop(0, lists_ref[which, 2 * MAXP], each_slot, found)

    picked_ref[0] = lax.fori_loop(0, LISTS, each_list, jnp.int32(0))


def tile_kernel(picked_ref, near_ref, far_ref, near_out, far_out, near_sum, far_sum):
    near_sum[...] = jnp.zeros_like(near_sum)
    far_sum[...] = jnp.zeros_like(far_sum)
    ones = (lax.broadcasted_iota(jnp.int32, (AUG - VEC, BS), 0) == 0).astype(jnp.bfloat16)

    def each_tile(number, carry):
        code = picked_ref[number + 1]
        same = code >> 8
        near = (code >> 4) & 15
        far = code & 15
        mirror = jnp.where(same == 1, 0.0, 1.0).astype(jnp.float32)
        far_embed = far_ref[far, :EMB, :]
        near_vec = jnp.concatenate([near_ref[near, EMB:, :], ones], axis=0)
        far_vec = jnp.concatenate([far_ref[far, EMB:, :], ones], axis=0)
        far_terms = None
        for half in range(2):
            cut = slice(half * 256, half * 256 + 256)
            scores = jnp.dot(
                near_ref[near, :EMB, cut], far_embed, preferred_element_type=jnp.float32
            )
            tile = (0.5 * jnp.tanh(scores) + 0.5).astype(jnp.bfloat16)
            near_terms = lax.dot_general(
                far_vec, tile, (((1,), (1,)), ((), ())), preferred_element_type=jnp.float32
            )
            near_sum[near, :, cut] += near_terms
            part = jnp.dot(near_vec[:, cut], tile, preferred_element_type=jnp.float32)
            far_terms = part if far_terms is None else far_terms + part
        far_sum[far] += far_terms * mirror
        return carry

    lax.fori_loop(0, picked_ref[0], each_tile, 0)
    near_out[...] = near_sum[...].astype(jnp.bfloat16)
    far_out[...] = far_sum[...].astype(jnp.bfloat16)


def on_device(embeddings, vectors, block_pairs, counts):
    score_scale = 0.5 / math.sqrt(EMB)
    vector_bf16 = vectors.astype(jnp.bfloat16)
    turned = embeddings.T
    near_send = jnp.concatenate(
        [
            jnp.concatenate([turned[:256], turned[256:]], axis=1)
            * jnp.asarray(score_scale, jnp.bfloat16),
            vector_bf16,
        ],
        axis=0,
    )
    far_send = jnp.concatenate([embeddings, vector_bf16], axis=0)
    near_all = lax.all_gather(near_send, NEAR)
    far_all = lax.all_to_all(
        jnp.broadcast_to(far_send[None], (WAYS,) + far_send.shape), FAR, 0, 0
    )
    own_list = jnp.concatenate(
        [block_pairs.reshape(-1), counts, jnp.zeros((128 - 2 * MAXP - 1,), jnp.int32)]
    )
    lists = lax.all_gather(own_list, ("k", "y"))
    place = jnp.stack([lax.axis_index("y"), lax.axis_index("k")]).astype(jnp.int32)
    smem = pl.BlockSpec(memory_space=pltpu.SMEM)
    vmem = pl.BlockSpec(memory_space=pltpu.VMEM)
    picked = pl.pallas_call(
        select_kernel,
        out_shape=jax.ShapeDtypeStruct((SLOTS,), jnp.int32),
        in_specs=[smem, smem],
        out_specs=smem,
        name="select_pairs",
    )(place, lists)
    near_part, far_part = pl.pallas_call(
        tile_kernel,
        out_shape=[jax.ShapeDtypeStruct((WAYS, AUG, BS), jnp.bfloat16)] * 2,
        in_specs=[smem, vmem, vmem],
        out_specs=[vmem, vmem],
        scratch_shapes=[pltpu.VMEM((WAYS, AUG, BS), jnp.float32)] * 2,
        compiler_params=pltpu.CompilerParams(vmem_limit_bytes=48 * 1024 * 1024),
        name="tiles",
    )(picked, near_all, far_all)
    near_back = lax.all_to_all(near_part, NEAR, 0, 0)
    far_back = lax.all_to_all(far_part, FAR, 0, 0)
    total = jnp.sum(near_back.astype(jnp.float32), axis=0) + jnp.sum(
        far_back.astype(jnp.float32), axis=0
    )
    walked = total[:VEC] / total[VEC : VEC + 1]
    points = BS * X * K * Z * Y
    local_gram = jnp.dot(
        walked, walked.T, precision=lax.Precision.HIGHEST, preferred_element_type=jnp.float32
    )
    partial_gram = local_gram.reshape(1, 8, 128)
    for group in (FAR, NEAR):
        shares = lax.all_to_all(jnp.broadcast_to(partial_gram, (WAYS, 8, 128)), group, 0, 0)
        partial_gram = jnp.sum(shares, axis=0, keepdims=True)
    gram_matrix = partial_gram.reshape(VEC, VEC) / points
    gram_factor = jnp.linalg.cholesky(gram_matrix)
    inverse = lax.linalg.triangular_solve(
        gram_factor, jnp.eye(VEC, dtype=jnp.float32), left_side=True, lower=True
    )
    embedding_basis = jnp.dot(
        inverse, walked, precision=lax.Precision.HIGHEST, preferred_element_type=jnp.float32
    )
    return (embedding_basis, gram_factor)


def solution(mesh):
    fine = Mesh(mesh.devices.reshape(X, K, Z, Y), EVERY)
    in_specs = (P(None, EVERY), P(None, EVERY), P(EVERY, None), P(EVERY))
    out_specs = (P(None, EVERY), P())
    return jax.shard_map(
        on_device, mesh=fine, in_specs=in_specs, out_specs=out_specs, check_vma=False
    )
```

```python
import functools
import math

import jax
import jax.numpy as jnp
from jax import lax
from jax.experimental import pallas as pl
from jax.experimental.pallas import tpu as pltpu
from jax.sharding import Mesh
from jax.sharding import PartitionSpec as P

X, K, Z, Y = 4, 2, 8, 4
COLS = Z * Y
NEAR = ("k", "z")
FAR = ("x", "y")
EVERY = ("x", "k", "z", "y")
WAYS = 16
BS = 512
EMB = 256
VEC = 32
AUG = 48
MAXP = 24
LISTS = K * Y
SLOTS = 256


def select_kernel(place_ref, lists_ref, picked_ref):
    own_y = place_ref[0]
    own_k = place_ref[1]

    def each_list(which, found):
        def each_slot(slot, found):
            row_block = lists_ref[which, 2 * slot]
            col_block = lists_ref[which, 2 * slot + 1]
            near = ((row_block >> 5) & 1) * Z + ((row_block >> 2) & 7)
            far = ((col_block >> 6) & 3) * Y + (col_block & 3)
            same = (row_block == col_block).astype(jnp.int32)
            mine = ((row_block & 3) == own_y) & (((col_block >> 5) & 1) == own_k)
            picked_ref[found + 1] = same * 256 + near * 16 + far
            return found + mine.astype(jnp.int32)

        return lax.fori_loop(0, lists_ref[which, 2 * MAXP], each_slot, found)

    picked_ref[0] = lax.fori_loop(0, LISTS, each_list, jnp.int32(0))


def tile_kernel(
    place_ref, picked_ref, near_ref, far_ref, keep_out, give_out, far_out, near_sum, far_sum
):
    near_sum[...] = jnp.zeros_like(near_sum)
    far_sum[...] = jnp.zeros_like(far_sum)
    ones = (lax.broadcasted_iota(jnp.int32, (AUG - VEC, BS), 0) == 0).astype(jnp.bfloat16)

    def each_tile(number, carry):
        code = picked_ref[number + 1]
        same = code >> 8
        near = (code >> 4) & 15
        far = code & 15
        mirror = jnp.where(same == 1, 0.0, 1.0).astype(jnp.float32)
        far_embed = far_ref[far, :EMB, :]
        near_vec = jnp.concatenate([near_ref[near, EMB:, :], ones], axis=0)
        far_vec = jnp.concatenate([far_ref[far, EMB:, :], ones], axis=0)
        far_terms = None
        for half in range(2):
            cut = slice(half * 256, half * 256 + 256)
            scores = jnp.dot(
                near_ref[near, :EMB, cut], far_embed, preferred_element_type=jnp.float32
            )
            tile = (0.5 * jnp.tanh(scores) + 0.5).astype(jnp.bfloat16)
            near_terms = lax.dot_general(
                far_vec, tile, (((1,), (1,)), ((), ())), preferred_element_type=jnp.float32
            )
            near_sum[near, :, cut] += near_terms
            part = jnp.dot(near_vec[:, cut], tile, preferred_element_type=jnp.float32)
            far_terms = part if far_terms is None else far_terms + part
        far_sum[far] += far_terms * mirror
        return carry

    lax.fori_loop(0, picked_ref[0], each_tile, 0)
    own_k = place_ref[1]
    keep_out[...] = near_sum[pl.ds(own_k * Z, Z)]
    give_out[...] = near_sum[pl.ds((1 - own_k) * Z, Z)].astype(jnp.bfloat16)
    far_out[...] = far_sum[...].astype(jnp.bfloat16)


def on_device(embeddings, vectors, block_pairs, counts):
    score_scale = 0.5 / math.sqrt(EMB)
    vector_bf16 = vectors.astype(jnp.bfloat16)
    turned = embeddings.T
    near_send = jnp.concatenate(
        [
            jnp.concatenate([turned[:256], turned[256:]], axis=1)
            * jnp.asarray(score_scale, jnp.bfloat16),
            vector_bf16,
        ],
        axis=0,
    )
    far_send = jnp.concatenate([embeddings, vector_bf16], axis=0)
    own_list = jnp.concatenate(
        [block_pairs.reshape(-1), counts, jnp.zeros((128 - 2 * MAXP - 1,), jnp.int32)]
    )
    other_list = lax.ppermute(own_list, "k", [(0, 1), (1, 0)])
    chip_lists = jnp.stack([own_list, other_list])
    lists = lax.all_to_all(jnp.broadcast_to(chip_lists[None], (Y, K, 128)), "y", 0, 0)
    lists, far_send = lax.optimization_barrier((lists.reshape(LISTS, 128), far_send))
    near_all = lax.all_gather(near_send, NEAR)
    far_all = lax.all_to_all(
        jnp.broadcast_to(far_send[None], (WAYS,) + far_send.shape), FAR, 0, 0
    )
    place = jnp.stack([lax.axis_index("y"), lax.axis_index("k")]).astype(jnp.int32)
    smem = pl.BlockSpec(memory_space=pltpu.SMEM)
    vmem = pl.BlockSpec(memory_space=pltpu.VMEM)
    picked = pl.pallas_call(
        select_kernel,
        out_shape=jax.ShapeDtypeStruct((SLOTS,), jnp.int32),
        in_specs=[smem, smem],
        out_specs=smem,
        name="select_pairs",
    )(place, lists)
    near_keep, near_give, far_part = pl.pallas_call(
        tile_kernel,
        out_shape=[
            jax.ShapeDtypeStruct((Z, AUG, BS), jnp.float32),
            jax.ShapeDtypeStruct((Z, AUG, BS), jnp.bfloat16),
            jax.ShapeDtypeStruct((WAYS, AUG, BS), jnp.bfloat16),
        ],
        in_specs=[smem, smem, vmem, vmem],
        out_specs=[vmem, vmem, vmem],
        scratch_shapes=[pltpu.VMEM((WAYS, AUG, BS), jnp.float32)] * 2,
        compiler_params=pltpu.CompilerParams(vmem_limit_bytes=48 * 1024 * 1024),
        name="tiles",
    )(place, picked, near_all, far_all)
    far_back = lax.all_to_all(far_part, FAR, 0, 0)
    near_taken = lax.ppermute(near_give, "k", [(0, 1), (1, 0)])
    near_pair = (near_keep + near_taken.astype(jnp.float32)).astype(jnp.bfloat16)
    near_back = lax.all_to_all(near_pair, "z", 0, 0)
    total = jnp.sum(near_back.astype(jnp.float32), axis=0) + jnp.sum(
        far_back.astype(jnp.float32), axis=0
    )
    walked = total[:VEC] / total[VEC : VEC + 1]
    points = BS * X * K * Z * Y
    local_gram = jnp.dot(
        walked, walked.T, precision=lax.Precision.HIGHEST, preferred_element_type=jnp.float32
    )
    partial_gram = local_gram.reshape(1, 8, 128)
    for group in (FAR, NEAR):
        shares = lax.all_to_all(jnp.broadcast_to(partial_gram, (WAYS, 8, 128)), group, 0, 0)
        partial_gram = jnp.sum(shares, axis=0, keepdims=True)
    gram_matrix = partial_gram.reshape(VEC, VEC) / points
    gram_factor = jnp.linalg.cholesky(gram_matrix)
    inverse = lax.linalg.triangular_solve(
        gram_factor, jnp.eye(VEC, dtype=jnp.float32), left_side=True, lower=True
    )
    embedding_basis = jnp.dot(
        inverse, walked, precision=lax.Precision.HIGHEST, preferred_element_type=jnp.float32
    )
    return (embedding_basis, gram_factor)


def solution(mesh):
    fine = Mesh(mesh.devices.reshape(X, K, Z, Y), EVERY)
    in_specs = (P(None, EVERY), P(None, EVERY), P(EVERY, None), P(EVERY))
    out_specs = (P(None, EVERY), P())
    return jax.shard_map(
        on_device, mesh=fine, in_specs=in_specs, out_specs=out_specs, check_vma=False
    )
```

```python
import functools
import math

import jax
import jax.numpy as jnp
from jax import lax
from jax.experimental import pallas as pl
from jax.experimental.pallas import tpu as pltpu
from jax.sharding import Mesh
from jax.sharding import PartitionSpec as P

X, K, Z, Y = 4, 2, 8, 4
COLS = Z * Y
NEAR = ("k", "z")
FAR = ("x", "y")
EVERY = ("x", "k", "z", "y")
WAYS = 16
BS = 512
EMB = 256
VEC = 32
AUG = 48
MAXP = 24
LISTS = K * Y
SLOTS = 256


def select_kernel(place_ref, lists_ref, picked_ref):
    own_y = place_ref[0]
    own_k = place_ref[1]
    own_z = place_ref[2]

    def each_list(which, found):
        def each_slot(slot, found):
            row_block = lists_ref[which, 2 * slot]
            col_block = lists_ref[which, 2 * slot + 1]
            core = (((row_block >> 5) & 1) ^ own_k) * Z
            row_z = (row_block >> 2) & 7
            apart = row_z ^ own_z
            near = core + ((row_z - own_z) & 7)
            back = core + (apart & 1) * 4 + (apart & 2) + (apart >> 2)
            far = ((col_block >> 6) & 3) * Y + (col_block & 3)
            same = (row_block == col_block).astype(jnp.int32)
            mine = ((row_block & 3) == own_y) & (((col_block >> 5) & 1) == own_k)
            picked_ref[found + 1] = ((same * 16 + back) * 16 + near) * 16 + far
            return found + mine.astype(jnp.int32)

        return lax.fori_loop(0, lists_ref[which, 2 * MAXP], each_slot, found)

    picked_ref[0] = lax.fori_loop(0, LISTS, each_list, jnp.int32(0))


def tile_kernel(picked_ref, far_hbm, *refs):
    near_hbm = refs[:WAYS]
    keep_out, give_out, far_out, near_ref, far_ref, near_sum, far_sum, sems = refs[WAYS:]
    copies = [pltpu.make_async_copy(far_hbm, far_ref, sems.at[WAYS])]
    for slot in range(WAYS):
        copies.append(pltpu.make_async_copy(near_hbm[slot], near_ref.at[slot], sems.at[slot]))
    for copy in copies:
        copy.start()
    near_sum[...] = jnp.zeros_like(near_sum)
    far_sum[...] = jnp.zeros_like(far_sum)
    ones = (lax.broadcasted_iota(jnp.int32, (AUG - VEC, BS), 0) == 0).astype(jnp.bfloat16)
    for copy in copies:
        copy.wait()

    def each_tile(number, carry):
        code = picked_ref[number + 1]
        back = (code >> 8) & 15
        near = (code >> 4) & 15
        far = code & 15
        mirror = jnp.where((code >> 12) == 1, 0.0, 1.0).astype(jnp.float32)
        far_embed = far_ref[far, :EMB, :]
        near_vec = jnp.concatenate([near_ref[near, EMB:, :], ones], axis=0)
        far_vec = jnp.concatenate([far_ref[far, EMB:, :], ones], axis=0)
        far_terms = None
        for half in range(2):
            cut = slice(half * 256, half * 256 + 256)
            scores = jnp.dot(
                near_ref[near, :EMB, cut], far_embed, preferred_element_type=jnp.float32
            )
            tile = (0.5 * jnp.tanh(scores) + 0.5).astype(jnp.bfloat16)
            near_terms = lax.dot_general(
                far_vec, tile, (((1,), (1,)), ((), ())), preferred_element_type=jnp.float32
            )
            near_sum[back, :, cut] += near_terms
            part = jnp.dot(near_vec[:, cut], tile, preferred_element_type=jnp.float32)
            far_terms = part if far_terms is None else far_terms + part
        far_sum[far] += far_terms * mirror
        return carry

    lax.fori_loop(0, picked_ref[0], each_tile, 0)
    keep_out[...] = near_sum[:Z]
    give_out[...] = near_sum[Z:].astype(jnp.bfloat16)
    far_out[...] = far_sum[...].astype(jnp.bfloat16)


def shift(values, axis, size, by):
    return lax.ppermute(values, axis, [(i, (i + by) % size) for i in range(size)])


def swap(values, axis, size, bit):
    return lax.ppermute(values, axis, [(i, i ^ bit) for i in range(size)])


def on_device(embeddings, vectors, block_pairs, counts):
    score_scale = 0.5 / math.sqrt(EMB)
    vector_bf16 = vectors.astype(jnp.bfloat16)
    turned = embeddings.T
    near_send = jnp.concatenate(
        [
            jnp.concatenate([turned[:256], turned[256:]], axis=1)
            * jnp.asarray(score_scale, jnp.bfloat16),
            vector_bf16,
        ],
        axis=0,
    )
    far_send = jnp.concatenate([embeddings, vector_bf16], axis=0)
    own_list = jnp.concatenate(
        [block_pairs.reshape(-1), counts, jnp.zeros((128 - 2 * MAXP - 1,), jnp.int32)]
    )
    chip_lists = jnp.stack([own_list, swap(own_list, "k", K, 1)])
    lists = jnp.concatenate([chip_lists] + [shift(chip_lists, "y", Y, by) for by in (1, 2, 3)])
    far_all = lax.all_gather(far_send, FAR)
    ring = {0: near_send}
    for step in range(1, Z // 2 + 1):
        ring[Z - step] = shift(ring[(Z - step + 1) % Z], "z", Z, 1)
        if step < Z // 2:
            ring[step] = shift(ring[step - 1], "z", Z, -1)
    near_blocks = [ring[i] for i in range(Z)]
    near_blocks += [swap(block, "k", K, 1) for block in near_blocks]
    place = jnp.stack([lax.axis_index(name) for name in ("y", "k", "z")]).astype(jnp.int32)
    smem = pl.BlockSpec(memory_space=pltpu.SMEM)
    vmem = pl.BlockSpec(memory_space=pltpu.VMEM)
    picked = pl.pallas_call(
        select_kernel,
        out_shape=jax.ShapeDtypeStruct((SLOTS,), jnp.int32),
        in_specs=[smem, smem],
        out_specs=smem,
        name="select_pairs",
    )(place, lists)
    near_keep, near_give, far_part = pl.pallas_call(
        tile_kernel,
        out_shape=[
            jax.ShapeDtypeStruct((Z, AUG, BS), jnp.float32),
            jax.ShapeDtypeStruct((Z, AUG, BS), jnp.bfloat16),
            jax.ShapeDtypeStruct((WAYS, AUG, BS), jnp.bfloat16),
        ],
        in_specs=[smem] + [pl.BlockSpec(memory_space=pl.ANY)] * (1 + WAYS),
        out_specs=[vmem, vmem, vmem],
        scratch_shapes=[pltpu.VMEM((WAYS, EMB + VEC, BS), jnp.bfloat16)] * 2
        + [pltpu.VMEM((WAYS, AUG, BS), jnp.float32)] * 2
        + [pltpu.SemaphoreType.DMA((WAYS + 1,))],
        compiler_params=pltpu.CompilerParams(vmem_limit_bytes=48 * 1024 * 1024),
        name="tiles",
    )(picked, far_all, *near_blocks)
    far_back = lax.all_to_all(far_part, FAR, 0, 0)
    near_total = near_keep + swap(near_give, "k", K, 1).astype(jnp.float32)
    for bit in (1, 2, 4):
        left = near_total.shape[0] // 2
        taken = swap(near_total[left:].astype(jnp.bfloat16), "z", Z, bit)
        near_total = near_total[:left] + taken.astype(jnp.float32)
    total = near_total[0] + jnp.sum(far_back.astype(jnp.float32), axis=0)
    walked = total[:VEC] / total[VEC : VEC + 1]
    points = BS * X * K * Z * Y
    local_gram = jnp.dot(
        walked, walked.T, precision=lax.Precision.HIGHEST, preferred_element_type=jnp.float32
    )
    partial_gram = local_gram.reshape(1, 8, 128)
    for group in (FAR, NEAR):
        shares = lax.all_to_all(jnp.broadcast_to(partial_gram, (WAYS, 8, 128)), group, 0, 0)
        partial_gram = jnp.sum(shares, axis=0, keepdims=True)
    gram_matrix = partial_gram.reshape(VEC, VEC) / points
    gram_factor = jnp.linalg.cholesky(gram_matrix)
    inverse = lax.linalg.triangular_solve(
        gram_factor, jnp.eye(VEC, dtype=jnp.float32), left_side=True, lower=True
    )
    embedding_basis = jnp.dot(
        inverse, walked, precision=lax.Precision.HIGHEST, preferred_element_type=jnp.float32
    )
    return (embedding_basis, gram_factor)


def solution(mesh):
    fine = Mesh(mesh.devices.reshape(X, K, Z, Y), EVERY)
    in_specs = (P(None, EVERY), P(None, EVERY), P(EVERY, None), P(EVERY))
    out_specs = (P(None, EVERY), P())
    return jax.shard_map(
        on_device, mesh=fine, in_specs=in_specs, out_specs=out_specs, check_vma=False
    )
```

```python
import functools
import math

import jax
import jax.numpy as jnp
from jax import lax
from jax.experimental import pallas as pl
from jax.experimental.pallas import tpu as pltpu
from jax.sharding import Mesh
from jax.sharding import PartitionSpec as P

X, K, U, W, Y = 4, 2, 4, 2, 4
Z = U * W
NEAR = ("k", "u", "w")
FAR = ("x", "y")
EVERY = ("x", "k", "u", "w", "y")
WAYS = 16
BS = 512
EMB = 256
VEC = 32
AUG = 48
FIRST = 192
MAXP = 24
LISTS = K * Y
SLOTS = 256


def select_kernel(place_ref, lists_ref, picked_ref):
    own_y = place_ref[0]
    own_k = place_ref[1]
    own_z = place_ref[2]

    def each_list(which, found):
        def each_slot(slot, found):
            row_block = lists_ref[which, 2 * slot]
            col_block = lists_ref[which, 2 * slot + 1]
            core = (((row_block >> 5) & 1) ^ own_k) * Z
            row_z = (row_block >> 2) & 7
            near = core + ((row_z - own_z) & 7)
            back = core + ((row_z ^ own_z) & 1) * U + (row_z >> 1)
            far = ((col_block >> 6) & 3) * Y + (col_block & 3)
            same = (row_block == col_block).astype(jnp.int32)
            mine = ((row_block & 3) == own_y) & (((col_block >> 5) & 1) == own_k)
            picked_ref[found + 1] = ((same * 16 + back) * 16 + near) * 16 + far
            return found + mine.astype(jnp.int32)

        return lax.fori_loop(0, lists_ref[which, 2 * MAXP], each_slot, found)

    picked_ref[0] = lax.fori_loop(0, LISTS, each_list, jnp.int32(0))


def tile_kernel(picked_ref, far_first, far_rest, *refs):
    near_hbm = refs[:WAYS]
    keep_out, give_out, far_out, near_ref, far_ref, near_sum, far_sum, sems = refs[WAYS:]
    copies = [
        pltpu.make_async_copy(far_first, far_ref.at[:, :FIRST, :], sems.at[WAYS]),
        pltpu.make_async_copy(far_rest, far_ref.at[:, FIRST:, :], sems.at[WAYS + 1]),
    ]
    for slot in range(WAYS):
        copies.append(pltpu.make_async_copy(near_hbm[slot], near_ref.at[slot], sems.at[slot]))
    for copy in copies:
        copy.start()
    near_sum[...] = jnp.zeros_like(near_sum)
    far_sum[...] = jnp.zeros_like(far_sum)
    ones = (lax.broadcasted_iota(jnp.int32, (AUG - VEC, BS), 0) == 0).astype(jnp.bfloat16)
    for copy in copies:
        copy.wait()

    def each_tile(number, carry):
        code = picked_ref[number + 1]
        back = (code >> 8) & 15
        near = (code >> 4) & 15
        far = code & 15
        mirror = jnp.where((code >> 12) == 1, 0.0, 1.0).astype(jnp.float32)
        far_embed = far_ref[far, :EMB, :]
        near_vec = jnp.concatenate([near_ref[near, EMB:, :], ones], axis=0)
        far_vec = jnp.concatenate([far_ref[far, EMB:, :], ones], axis=0)
        far_terms = None
        for half in range(2):
            cut = slice(half * 256, half * 256 + 256)
            scores = jnp.dot(
                near_ref[near, :EMB, cut], far_embed, preferred_element_type=jnp.float32
            )
            tile = (0.5 * jnp.tanh(scores) + 0.5).astype(jnp.bfloat16)
            near_terms = lax.dot_general(
                far_vec, tile, (((1,), (1,)), ((), ())), preferred_element_type=jnp.float32
            )
            near_sum[back, :, cut] += near_terms
            part = jnp.dot(near_vec[:, cut], tile, preferred_element_type=jnp.float32)
            far_terms = part if far_terms is None else far_terms + part
        far_sum[far] += far_terms * mirror
        return carry

    lax.fori_loop(0, picked_ref[0], each_tile, 0)
    keep_out[...] = near_sum[:Z]
    give_out[...] = near_sum[Z:].astype(jnp.bfloat16)
    far_out[...] = far_sum[...].astype(jnp.bfloat16)


def finish_kernel(gram_ref, walked_ref, basis_out, factor_out, wide_ref):
    row = lax.broadcasted_iota(jnp.int32, (VEC, 128), 0)
    lane = lax.broadcasted_iota(jnp.int32, (VEC, 128), 1)
    wide_ref[...] = (lane == row + VEC).astype(jnp.float32)
    wide_ref[:, :VEC] = gram_ref[...]
    wide = wide_ref[...]
    factor = jnp.zeros((VEC, 128), jnp.float32)
    for step in range(VEC):
        pivot = wide[step : step + 1, step : step + 1]
        root = lax.rsqrt(pivot)
        root = root * (1.5 - 0.5 * pivot * root * root)
        scaled = wide[step : step + 1, :] * root
        column = jnp.broadcast_to(wide[:, step : step + 1] * root, (VEC, 128))
        factor = jnp.where((lane == step) & (row >= step), column, factor)
        lower = jnp.where(row > step, wide - column * scaled, wide)
        wide = jnp.where(row == step, jnp.broadcast_to(scaled, (VEC, 128)), lower)
    wide_ref[...] = wide
    basis_out[...] = jnp.dot(
        wide_ref[:, VEC : 2 * VEC],
        walked_ref[...],
        precision=lax.Precision.HIGHEST,
        preferred_element_type=jnp.float32,
    )
    factor_out[...] = factor[:, :VEC]


def shift(values, axis, size, by):
    return lax.ppermute(values, axis, [(i, (i + by) % size) for i in range(size)])


def swap(values, axis, size, bit):
    return lax.ppermute(values, axis, [(i, i ^ bit) for i in range(size)])


def on_device(embeddings, vectors, block_pairs, counts):
    score_scale = 0.5 / math.sqrt(EMB)
    vector_bf16 = vectors.astype(jnp.bfloat16)
    turned = embeddings.T
    near_send = jnp.concatenate(
        [
            jnp.concatenate([turned[:256], turned[256:]], axis=1)
            * jnp.asarray(score_scale, jnp.bfloat16),
            vector_bf16,
        ],
        axis=0,
    )
    far_tail = jnp.concatenate([embeddings[FIRST:], vector_bf16], axis=0)
    own_list = jnp.concatenate(
        [block_pairs.reshape(-1), counts, jnp.zeros((128 - 2 * MAXP - 1,), jnp.int32)]
    )
    chip_lists = jnp.stack([own_list, swap(own_list, "k", K, 1)])
    lists = jnp.concatenate([chip_lists] + [shift(chip_lists, "y", Y, by) for by in (1, 2, 3)])
    far_first = lax.all_gather(embeddings[:FIRST], FAR)
    far_rest = lax.all_to_all(
        jnp.broadcast_to(far_tail[None], (WAYS,) + far_tail.shape), FAR, 0, 0
    )
    ring = {0: near_send}
    for step in range(1, Z // 2 + 1):
        ring[Z - step] = shift(ring[(Z - step + 1) % Z], ("u", "w"), Z, 1)
        if step < Z // 2:
            ring[step] = shift(ring[step - 1], ("u", "w"), Z, -1)
    near_blocks = [ring[i] for i in range(Z)]
    near_blocks += [swap(block, "k", K, 1) for block in near_blocks]
    place = jnp.stack([lax.axis_index(name) for name in ("y", "k", ("u", "w"))]).astype(jnp.int32)
    smem = pl.BlockSpec(memory_space=pltpu.SMEM)
    vmem = pl.BlockSpec(memory_space=pltpu.VMEM)
    picked = pl.pallas_call(
        select_kernel,
        out_shape=jax.ShapeDtypeStruct((SLOTS,), jnp.int32),
        in_specs=[smem, smem],
        out_specs=smem,
        name="select_pairs",
    )(place, lists)
    near_keep, near_give, far_part = pl.pallas_call(
        tile_kernel,
        out_shape=[
            jax.ShapeDtypeStruct((Z, AUG, BS), jnp.float32),
            jax.ShapeDtypeStruct((Z, AUG, BS), jnp.bfloat16),
            jax.ShapeDtypeStruct((WAYS, AUG, BS), jnp.bfloat16),
        ],
        in_specs=[smem] + [pl.BlockSpec(memory_space=pl.ANY)] * (2 + WAYS),
        out_specs=[vmem, vmem, vmem],
        scratch_shapes=[pltpu.VMEM((WAYS, EMB + VEC, BS), jnp.bfloat16)] * 2
        + [pltpu.VMEM((WAYS, AUG, BS), jnp.float32)] * 2
        + [pltpu.SemaphoreType.DMA((WAYS + 2,))],
        compiler_params=pltpu.CompilerParams(vmem_limit_bytes=48 * 1024 * 1024),
        name="tiles",
    )(picked, far_first, far_rest, *near_blocks)
    far_back = lax.all_to_all(far_part, FAR, 0, 0)
    near_total = near_keep + swap(near_give, "k", K, 1).astype(jnp.float32)
    near_taken = swap(near_total[U:].astype(jnp.bfloat16), "w", W, 1)
    near_total = (near_total[:U] + near_taken.astype(jnp.float32)).astype(jnp.bfloat16)
    near_back = lax.all_to_all(near_total, "u", 0, 0)
    total = jnp.sum(near_back.astype(jnp.float32), axis=0) + jnp.sum(
        far_back.astype(jnp.float32), axis=0
    )
    walked = total[:VEC] / total[VEC : VEC + 1]
    points = BS * X * K * Z * Y
    local_gram = jnp.dot(
        walked, walked.T, precision=lax.Precision.HIGHEST, preferred_element_type=jnp.float32
    )
    partial_gram = local_gram.reshape(1, 8, 128)
    for group in (FAR, NEAR):
        shares = lax.all_to_all(jnp.broadcast_to(partial_gram, (WAYS, 8, 128)), group, 0, 0)
        partial_gram = jnp.sum(shares, axis=0, keepdims=True)
    gram_matrix = partial_gram.reshape(VEC, VEC) / points
    embedding_basis, gram_factor = pl.pallas_call(
        finish_kernel,
        out_shape=[
            jax.ShapeDtypeStruct((VEC, BS), jnp.float32),
            jax.ShapeDtypeStruct((VEC, VEC), jnp.float32),
        ],
        in_specs=[vmem, vmem],
        out_specs=[vmem, vmem],
        scratch_shapes=[pltpu.VMEM((VEC, 128), jnp.float32)],
        name="finish",
    )(gram_matrix, walked)
    return (embedding_basis, gram_factor)


def solution(mesh):
    fine = Mesh(mesh.devices.reshape(X, K, U, W, Y), EVERY)
    in_specs = (P(None, EVERY), P(None, EVERY), P(EVERY, None), P(EVERY))
    out_specs = (P(None, EVERY), P())
    return jax.shard_map(
        on_device, mesh=fine, in_specs=in_specs, out_specs=out_specs, check_vma=False
    )
```

```python
import functools
import math

import jax
import jax.numpy as jnp
from jax import lax
from jax.experimental import pallas as pl
from jax.experimental.pallas import tpu as pltpu
from jax.sharding import Mesh
from jax.sharding import PartitionSpec as P

X, K, Z, Y = 4, 2, 8, 4
FAR = ("x", "k", "y")
EVERY = ("x", "k", "z", "y")
FARS = X * K * Y
BS = 512
EMB = 256
VEC = 32
AUG = 48
MAXP = 24
SLOTS = 128


def select_kernel(place_ref, lists_ref, picked_ref):
    own_y = place_ref[0]
    own_k = place_ref[1]
    own_z = place_ref[2]

    def each_list(which, found):
        def each_slot(slot, found):
            row_block = lists_ref[which, 2 * slot]
            col_block = lists_ref[which, 2 * slot + 1]
            row_z = (row_block >> 2) & 7
            near = (row_z - own_z) & 7
            apart = row_z ^ own_z
            back = (apart & 1) * 4 + (apart & 2) + (apart >> 2)
            col_row = col_block >> 5
            far = col_row * Y + (col_block & 3)
            home = ((col_row & 1) ^ own_k) * (X * Y) + (col_row >> 1) * Y + (col_block & 3)
            same = (row_block == col_block).astype(jnp.int32)
            picked_ref[found + 1] = (((same * 8 + back) * 8 + near) * FARS + home) * FARS + far
            return found + ((row_block & 3) == own_y).astype(jnp.int32)

        return lax.fori_loop(0, lists_ref[which, 2 * MAXP], each_slot, found)

    picked_ref[0] = lax.fori_loop(0, Y, each_list, jnp.int32(0))


def tile_kernel(picked_ref, far_hbm, *refs):
    near_hbm = refs[:Z]
    near_keep, near_give, far_keep, far_give, near_ref, far_ref, near_sum, far_sum, sems = refs[Z:]
    copies = [pltpu.make_async_copy(far_hbm, far_ref, sems.at[Z])]
    for slot in range(Z):
        copies.append(pltpu.make_async_copy(near_hbm[slot], near_ref.at[slot], sems.at[slot]))
    for copy in copies:
        copy.start()
    near_sum[...] = jnp.zeros_like(near_sum)
    far_sum[...] = jnp.zeros_like(far_sum)
    ones = (lax.broadcasted_iota(jnp.int32, (AUG - VEC, BS), 0) == 0).astype(jnp.bfloat16)
    for copy in copies:
        copy.wait()

    def each_tile(number, carry):
        code = picked_ref[number + 1]
        far = code & 31
        home = (code >> 5) & 31
        near = (code >> 10) & 7
        back = (code >> 13) & 7
        mirror = jnp.where((code >> 16) == 1, 0.0, 1.0).astype(jnp.float32)
        far_embed = far_ref[far, :EMB, :]
        near_vec = jnp.concatenate([near_ref[near, EMB:, :], ones], axis=0)
        far_vec = jnp.concatenate([far_ref[far, EMB:, :], ones], axis=0)
        far_terms = None
        for half in range(2):
            cut = slice(half * 256, half * 256 + 256)
            scores = jnp.dot(
                near_ref[near, :EMB, cut], far_embed, preferred_element_type=jnp.float32
            )
            tile = (0.5 * jnp.tanh(scores) + 0.5).astype(jnp.bfloat16)
            near_terms = lax.dot_general(
                far_vec, tile, (((1,), (1,)), ((), ())), preferred_element_type=jnp.float32
            )
            near_sum[back, :, cut] += near_terms
            part = jnp.dot(near_vec[:, cut], tile, preferred_element_type=jnp.float32)
            far_terms = part if far_terms is None else far_terms + part
        far_sum[home] += far_terms * mirror
        return carry

    lax.fori_loop(0, picked_ref[0], each_tile, 0)
    near_keep[...] = near_sum[: Z // 2]
    near_give[...] = near_sum[Z // 2 :].astype(jnp.bfloat16)
    far_keep[...] = far_sum[: X * Y]
    far_give[...] = far_sum[X * Y :].astype(jnp.bfloat16)


def finish_kernel(gram_ref, walked_ref, basis_out, factor_out, wide_ref):
    row = lax.broadcasted_iota(jnp.int32, (VEC, 128), 0)
    lane = lax.broadcasted_iota(jnp.int32, (VEC, 128), 1)
    wide_ref[...] = (lane == row + VEC).astype(jnp.float32)
    wide_ref[:, :VEC] = gram_ref[...]
    wide = wide_ref[...]
    factor = jnp.zeros((VEC, 128), jnp.float32)
    for step in range(VEC):
        pivot = wide[step : step + 1, step : step + 1]
        root = lax.rsqrt(pivot)
        root = root * (1.5 - 0.5 * pivot * root * root)
        scaled = wide[step : step + 1, :] * root
        column = jnp.broadcast_to(wide[:, step : step + 1] * root, (VEC, 128))
        factor = jnp.where((lane == step) & (row >= step), column, factor)
        lower = jnp.where(row > step, wide - column * scaled, wide)
        wide = jnp.where(row == step, jnp.broadcast_to(scaled, (VEC, 128)), lower)
    wide_ref[...] = wide
    basis_out[...] = jnp.dot(
        wide_ref[:, VEC : 2 * VEC],
        walked_ref[...],
        precision=lax.Precision.HIGHEST,
        preferred_element_type=jnp.float32,
    )
    factor_out[...] = factor[:, :VEC]


def shift(values, axis, size, by):
    return lax.ppermute(values, axis, [(i, (i + by) % size) for i in range(size)])


def swap(values, axis, size, bit):
    return lax.ppermute(values, axis, [(i, i ^ bit) for i in range(size)])


def on_device(embeddings, vectors, block_pairs, counts):
    score_scale = 0.5 / math.sqrt(EMB)
    vector_bf16 = vectors.astype(jnp.bfloat16)
    far_send = lax.optimization_barrier(jnp.concatenate([embeddings, vector_bf16], axis=0))
    far_all = lax.all_gather(far_send, FAR)
    turned = embeddings.T
    near_send = jnp.concatenate(
        [
            jnp.concatenate([turned[:256], turned[256:]], axis=1)
            * jnp.asarray(score_scale, jnp.bfloat16),
            vector_bf16,
        ],
        axis=0,
    )
    ring = {0: near_send}
    for step in range(1, Z // 2 + 1):
        ring[Z - step] = shift(ring[(Z - step + 1) % Z], "z", Z, 1)
        if step < Z // 2:
            ring[step] = shift(ring[step - 1], "z", Z, -1)
    near_blocks = [ring[i] for i in range(Z)]
    own_list = jnp.concatenate(
        [block_pairs.reshape(-1), counts, jnp.zeros((128 - 2 * MAXP - 1,), jnp.int32)]
    )
    lists = jnp.stack([own_list] + [shift(own_list, "y", Y, by) for by in (1, 2, 3)])
    place = jnp.stack([lax.axis_index(name) for name in ("y", "k", "z")]).astype(jnp.int32)
    smem = pl.BlockSpec(memory_space=pltpu.SMEM)
    vmem = pl.BlockSpec(memory_space=pltpu.VMEM)
    picked = pl.pallas_call(
        select_kernel,
        out_shape=jax.ShapeDtypeStruct((SLOTS,), jnp.int32),
        in_specs=[smem, smem],
        out_specs=smem,
        name="select_pairs",
    )(place, lists)
    near_total, near_give, far_total, far_give = pl.pallas_call(
        tile_kernel,
        out_shape=[
            jax.ShapeDtypeStruct((Z // 2, AUG, BS), jnp.float32),
            jax.ShapeDtypeStruct((Z // 2, AUG, BS), jnp.bfloat16),
            jax.ShapeDtypeStruct((X * Y, AUG, BS), jnp.float32),
            jax.ShapeDtypeStruct((X * Y, AUG, BS), jnp.bfloat16),
        ],
        in_specs=[smem] + [pl.BlockSpec(memory_space=pl.ANY)] * (1 + Z),
        out_specs=[vmem] * 4,
        scratch_shapes=[
            pltpu.VMEM((Z, EMB + VEC, BS), jnp.bfloat16),
            pltpu.VMEM((FARS, EMB + VEC, BS), jnp.bfloat16),
            pltpu.VMEM((Z, AUG, BS), jnp.float32),
            pltpu.VMEM((FARS, AUG, BS), jnp.float32),
            pltpu.SemaphoreType.DMA((Z + 1,)),
        ],
        compiler_params=pltpu.CompilerParams(vmem_limit_bytes=48 * 1024 * 1024),
        name="tiles",
    )(picked, far_all, *near_blocks)
    far_taken = swap(far_give, "k", K, 1)
    far_pair = (far_total + far_taken.astype(jnp.float32)).astype(jnp.bfloat16)
    far_back = lax.all_to_all(far_pair, ("x", "y"), 0, 0)
    for bit in (1, 2, 4):
        left = near_total.shape[0] if bit == 1 else near_total.shape[0] // 2
        give = near_give if bit == 1 else near_total[left:].astype(jnp.bfloat16)
        near_total = near_total[:left] + swap(give, "z", Z, bit).astype(jnp.float32)
    total = near_total[0] + jnp.sum(far_back.astype(jnp.float32), axis=0)
    walked = total[:VEC] / total[VEC : VEC + 1]
    points = BS * X * K * Z * Y
    local_gram = jnp.dot(
        walked, walked.T, precision=lax.Precision.HIGHEST, preferred_element_type=jnp.float32
    )
    partial_gram = local_gram.reshape(1, 8, 128)
    for group in (("x", "y"), ("k", "z")):
        shares = lax.all_to_all(jnp.broadcast_to(partial_gram, (16, 8, 128)), group, 0, 0)
        partial_gram = jnp.sum(shares, axis=0, keepdims=True)
    gram_matrix = partial_gram.reshape(VEC, VEC) / points
    embedding_basis, gram_factor = pl.pallas_call(
        finish_kernel,
        out_shape=[
            jax.ShapeDtypeStruct((VEC, BS), jnp.float32),
            jax.ShapeDtypeStruct((VEC, VEC), jnp.float32),
        ],
        in_specs=[vmem, vmem],
        out_specs=[vmem, vmem],
        scratch_shapes=[pltpu.VMEM((VEC, 128), jnp.float32)],
        name="finish",
    )(gram_matrix, walked)
    return (embedding_basis, gram_factor)


def solution(mesh):
    fine = Mesh(mesh.devices.reshape(X, K, Z, Y), EVERY)
    in_specs = (P(None, EVERY), P(None, EVERY), P(EVERY, None), P(EVERY))
    out_specs = (P(None, EVERY), P())
    return jax.shard_map(
        on_device, mesh=fine, in_specs=in_specs, out_specs=out_specs, check_vma=False
    )
```

```python
import functools
import math

import jax
import jax.numpy as jnp
from jax import lax
from jax.experimental import pallas as pl
from jax.experimental.pallas import tpu as pltpu
from jax.sharding import Mesh
from jax.sharding import PartitionSpec as P

X, K, Z, Y = 4, 2, 8, 4
FAR = ("x", "k", "y")
EVERY = ("x", "k", "z", "y")
FARS = X * K * Y
BS = 512
EMB = 256
HALF = 256
VEC = 32
AUG = 48
MAXP = 24
SLOTS = 128


def select_kernel(place_ref, lists_ref, picked_ref):
    own_y = place_ref[0]
    own_k = place_ref[1]
    own_z = place_ref[2]

    def each_list(which, found):
        def each_slot(slot, found):
            row_block = lists_ref[which, 2 * slot]
            col_block = lists_ref[which, 2 * slot + 1]
            row_z = (row_block >> 2) & 7
            near = (row_z - own_z) & 7
            apart = row_z ^ own_z
            back = (apart & 1) * 4 + (apart & 2) + (apart >> 2)
            col_row = col_block >> 5
            far = col_row * Y + (col_block & 3)
            home = ((col_row & 1) ^ own_k) * (X * Y) + (col_row >> 1) * Y + (col_block & 3)
            same = (row_block == col_block).astype(jnp.int32)
            picked_ref[found + 1] = (((same * 8 + back) * 8 + near) * FARS + home) * FARS + far
            return found + ((row_block & 3) == own_y).astype(jnp.int32)

        return lax.fori_loop(0, lists_ref[which, 2 * MAXP], each_slot, found)

    picked_ref[0] = lax.fori_loop(0, Y, each_list, jnp.int32(0))


def tile_kernel(last, picked_ref, far_hbm, *refs):
    near_hbm, refs = refs[:Z], refs[Z:]
    if last:
        near_before, near_keep, near_give, far_keep, far_give = refs[:5]
        near_ref, far_ref, near_sum, far_sum, sems = refs[5:]
    else:
        near_sum, far_keep, far_give, near_ref, far_ref, far_sum, sems = refs
    copies = [pltpu.make_async_copy(far_hbm, far_ref, sems.at[Z])]
    for slot in range(Z):
        copies.append(pltpu.make_async_copy(near_hbm[slot], near_ref.at[slot], sems.at[slot]))
    for copy in copies:
        copy.start()
    near_sum[...] = near_before[...] if last else jnp.zeros_like(near_sum)
    far_sum[...] = jnp.zeros_like(far_sum)
    ones = (lax.broadcasted_iota(jnp.int32, (AUG - VEC, BS), 0) == 0).astype(jnp.bfloat16)
    for copy in copies:
        copy.wait()
    found = picked_ref[0]

    def one_tile(number):
        live = number < found
        code = jnp.where(live, picked_ref[number + 1], 0)
        far = code & 31
        home = (code >> 5) & 31
        near = (code >> 10) & 7
        back = (code >> 13) & 7
        keep = jnp.where(live, 1.0, 0.0).astype(jnp.float32)
        mirror = jnp.where(live & ((code >> 16) == 0), 1.0, 0.0).astype(jnp.float32)
        near_vec = jnp.concatenate([near_ref[near, EMB:, :], ones], axis=0)
        far_vec = jnp.concatenate([far_ref[far, EMB:, :], ones[:, :HALF]], axis=0)
        scores = jnp.dot(
            far_ref[far, :EMB, :], near_ref[near, :EMB, :], preferred_element_type=jnp.float32
        )
        tile = (0.5 * jnp.tanh(scores) + 0.5).astype(jnp.bfloat16)
        far_terms = lax.dot_general(
            near_vec, tile, (((1,), (1,)), ((), ())), preferred_element_type=jnp.float32
        )
        near_terms = jnp.dot(far_vec, tile, preferred_element_type=jnp.float32)
        return back, near_terms * keep, home, far_terms * mirror

    def each_pair(number, carry):
        for back, near_terms, home, far_terms in [one_tile(2 * number), one_tile(2 * number + 1)]:
            near_sum[back] += near_terms
            far_sum[home] += far_terms
        return carry

    lax.fori_loop(0, (found + 1) >> 1, each_pair, 0)
    if last:
        near_keep[...] = near_sum[: Z // 2]
        near_give[...] = near_sum[Z // 2 :].astype(jnp.bfloat16)
    far_keep[...] = far_sum[: X * Y]
    far_give[...] = far_sum[X * Y :].astype(jnp.bfloat16)


def finish_kernel(gram_ref, walked_ref, basis_out, factor_out, wide_ref):
    row = lax.broadcasted_iota(jnp.int32, (VEC, 128), 0)
    lane = lax.broadcasted_iota(jnp.int32, (VEC, 128), 1)
    wide_ref[...] = (lane == row + VEC).astype(jnp.float32)
    wide_ref[:, :VEC] = gram_ref[...]
    wide = wide_ref[...]
    factor = jnp.zeros((VEC, 128), jnp.float32)
    for step in range(VEC):
        pivot = wide[step : step + 1, step : step + 1]
        root = lax.rsqrt(pivot)
        root = root * (1.5 - 0.5 * pivot * root * root)
        scaled = wide[step : step + 1, :] * root
        column = jnp.broadcast_to(wide[:, step : step + 1] * root, (VEC, 128))
        factor = jnp.where((lane == step) & (row >= step), column, factor)
        lower = jnp.where(row > step, wide - column * scaled, wide)
        wide = jnp.where(row == step, jnp.broadcast_to(scaled, (VEC, 128)), lower)
    wide_ref[...] = wide
    basis_out[...] = jnp.dot(
        wide_ref[:, VEC : 2 * VEC],
        walked_ref[...],
        precision=lax.Precision.HIGHEST,
        preferred_element_type=jnp.float32,
    )
    factor_out[...] = factor[:, :VEC]


def shift(values, axis, size, by):
    return lax.ppermute(values, axis, [(i, (i + by) % size) for i in range(size)])


def swap(values, axis, size, bit):
    return lax.ppermute(values, axis, [(i, i ^ bit) for i in range(size)])


def on_device(embeddings, vectors, block_pairs, counts):
    score_scale = 0.5 / math.sqrt(EMB)
    vector_bf16 = vectors.astype(jnp.bfloat16)
    turned = embeddings.T * jnp.asarray(score_scale, jnp.bfloat16)
    far_halves = []
    for cut in (slice(0, HALF), slice(HALF, BS)):
        far_send = jnp.concatenate([turned[cut], vector_bf16[:, cut]], axis=0)
        far_halves.append(lax.all_gather(far_send, FAR))
    near_send = jnp.concatenate([embeddings, vector_bf16], axis=0)
    ring = {0: near_send}
    for step in range(1, Z // 2 + 1):
        ring[Z - step] = shift(ring[(Z - step + 1) % Z], "z", Z, 1)
        if step < Z // 2:
            ring[step] = shift(ring[step - 1], "z", Z, -1)
    near_blocks = [ring[i] for i in range(Z)]
    own_list = jnp.concatenate(
        [block_pairs.reshape(-1), counts, jnp.zeros((128 - 2 * MAXP - 1,), jnp.int32)]
    )
    lists = jnp.stack([own_list] + [shift(own_list, "y", Y, by) for by in (1, 2, 3)])
    place = jnp.stack([lax.axis_index(name) for name in ("y", "k", "z")]).astype(jnp.int32)
    smem = pl.BlockSpec(memory_space=pltpu.SMEM)
    vmem = pl.BlockSpec(memory_space=pltpu.VMEM)
    picked = pl.pallas_call(
        select_kernel,
        out_shape=jax.ShapeDtypeStruct((SLOTS,), jnp.int32),
        in_specs=[smem, smem],
        out_specs=smem,
        name="select_pairs",
    )(place, lists)
    far_outs = [
        jax.ShapeDtypeStruct((X * Y, AUG, HALF), jnp.float32),
        jax.ShapeDtypeStruct((X * Y, AUG, HALF), jnp.bfloat16),
    ]
    whole_near = jax.ShapeDtypeStruct((Z, AUG, BS), jnp.float32)
    half_near = [
        jax.ShapeDtypeStruct((Z // 2, AUG, BS), jnp.float32),
        jax.ShapeDtypeStruct((Z // 2, AUG, BS), jnp.bfloat16),
    ]
    near_before = []
    far_pairs = []
    for last in (False, True):
        outs = (half_near if last else [whole_near]) + far_outs
        held = [pltpu.VMEM((Z, AUG, BS), jnp.float32)] if last else []
        results = pl.pallas_call(
            functools.partial(tile_kernel, last),
            out_shape=outs,
            in_specs=[smem]
            + [pl.BlockSpec(memory_space=pl.ANY)] * (1 + Z)
            + [vmem] * len(near_before),
            out_specs=[vmem] * len(outs),
            scratch_shapes=[
                pltpu.VMEM((Z, EMB + VEC, BS), jnp.bfloat16),
                pltpu.VMEM((FARS, EMB + VEC, HALF), jnp.bfloat16),
            ]
            + held
            + [
                pltpu.VMEM((FARS, AUG, HALF), jnp.float32),
                pltpu.SemaphoreType.DMA((Z + 1,)),
            ],
            compiler_params=pltpu.CompilerParams(vmem_limit_bytes=48 * 1024 * 1024),
            name="tiles_last" if last else "tiles_first",
        )(picked, far_halves[last], *near_blocks, *near_before)
        near_before = list(results[:-2])
        far_taken = swap(results[-1], "k", K, 1)
        far_pairs.append((results[-2] + far_taken.astype(jnp.float32)).astype(jnp.bfloat16))
    near_total, near_give = near_before
    far_pair = jnp.concatenate(far_pairs, axis=2)
    far_back = lax.all_to_all(far_pair, ("x", "y"), 0, 0)
    for bit in (1, 2, 4):
        left = near_total.shape[0] if bit == 1 else near_total.shape[0] // 2
        give = near_give if bit == 1 else near_total[left:].astype(jnp.bfloat16)
        near_total = near_total[:left] + swap(give, "z", Z, bit).astype(jnp.float32)
    total = near_total[0] + jnp.sum(far_back.astype(jnp.float32), axis=0)
    walked = total[:VEC] / total[VEC : VEC + 1]
    points = BS * X * K * Z * Y
    local_gram = jnp.dot(
        walked, walked.T, precision=lax.Precision.HIGHEST, preferred_element_type=jnp.float32
    )
    partial_gram = local_gram.reshape(1, 8, 128)
    for group in (("x", "y"), ("k", "z")):
        shares = lax.all_to_all(jnp.broadcast_to(partial_gram, (16, 8, 128)), group, 0, 0)
        partial_gram = jnp.sum(shares, axis=0, keepdims=True)
    gram_matrix = partial_gram.reshape(VEC, VEC) / points
    embedding_basis, gram_factor = pl.pallas_call(
        finish_kernel,
        out_shape=[
            jax.ShapeDtypeStruct((VEC, BS), jnp.float32),
            jax.ShapeDtypeStruct((VEC, VEC), jnp.float32),
        ],
        in_specs=[vmem, vmem],
        out_specs=[vmem, vmem],
        scratch_shapes=[pltpu.VMEM((VEC, 128), jnp.float32)],
        name="finish",
    )(gram_matrix, walked)
    return (embedding_basis, gram_factor)


def solution(mesh):
    fine = Mesh(mesh.devices.reshape(X, K, Z, Y), EVERY)
    in_specs = (P(None, EVERY), P(None, EVERY), P(EVERY, None), P(EVERY))
    out_specs = (P(None, EVERY), P())
    return jax.shard_map(
        on_device, mesh=fine, in_specs=in_specs, out_specs=out_specs, check_vma=False
    )
```

```python
import functools
import math

import jax
import jax.numpy as jnp
from jax import lax
from jax.experimental import pallas as pl
from jax.experimental.pallas import tpu as pltpu
from jax.sharding import Mesh
from jax.sharding import PartitionSpec as P

X, K, Z, Y = 4, 2, 8, 4
FAR = ("x", "k", "y")
EVERY = ("x", "k", "z", "y")
FARS = X * K * Y
BS = 512
EMB = 256
VEC = 32
AUG = 48
MAXP = 24
SLOTS = 128
PAIR = 2
AHEAD = 2


def select_kernel(place_ref, lists_ref, picked_ref):
    own_y = place_ref[0]
    own_k = place_ref[1]
    own_z = place_ref[2]

    def each_list(which, found):
        def each_slot(slot, found):
            row_block = lists_ref[which, 2 * slot]
            col_block = lists_ref[which, 2 * slot + 1]
            row_z = (row_block >> 2) & 7
            near = (row_z - own_z) & 7
            apart = row_z ^ own_z
            back = (apart & 1) * 4 + (apart & 2) + (apart >> 2)
            col_row = col_block >> 5
            far = col_row * Y + (col_block & 3)
            home = ((col_row & 1) ^ own_k) * (X * Y) + (col_row >> 1) * Y + (col_block & 3)
            same = (row_block == col_block).astype(jnp.int32)
            picked_ref[found + 1] = (((same * 8 + back) * 8 + near) * FARS + home) * FARS + far
            return found + ((row_block & 3) == own_y).astype(jnp.int32)

        return lax.fori_loop(0, lists_ref[which, 2 * MAXP], each_slot, found)

    picked_ref[0] = lax.fori_loop(0, Y, each_list, jnp.int32(0))


def tile_kernel(picked_ref, far_hbm, *refs):
    near_hbm = refs[:Z]
    near_keep, near_give, far_keep, far_give, near_ref, far_ref, near_sum, far_sum, sems = refs[Z:]
    found = picked_ref[0]

    def code_of(number):
        return jnp.where(number < found, picked_ref[number + 1], 0)

    def fetches(step):
        ring = lax.rem(step, AHEAD + 1) * PAIR
        return [
            pltpu.make_async_copy(
                far_hbm.at[code_of(step * PAIR + lane) & 31],
                far_ref.at[ring + lane],
                sems.at[Z + ring + lane],
            )
            for lane in range(PAIR)
        ]

    copies = [
        pltpu.make_async_copy(near_hbm[slot], near_ref.at[slot], sems.at[slot]) for slot in range(Z)
    ]
    for copy in copies:
        copy.start()
    for step in range(AHEAD):
        for copy in fetches(jnp.int32(step)):
            copy.start()
    near_sum[...] = jnp.zeros_like(near_sum)
    far_sum[...] = jnp.zeros_like(far_sum)
    ones = (lax.broadcasted_iota(jnp.int32, (AUG - VEC, BS), 0) == 0).astype(jnp.bfloat16)
    for copy in copies:
        copy.wait()

    def one_tile(step, lane):
        number = step * PAIR + lane
        live = number < found
        code = code_of(number)
        far = lax.rem(step, AHEAD + 1) * PAIR + lane
        home = (code >> 5) & 31
        near = (code >> 10) & 7
        back = (code >> 13) & 7
        keep = jnp.where(live, 1.0, 0.0).astype(jnp.float32)
        mirror = jnp.where(live & ((code >> 16) == 0), 1.0, 0.0).astype(jnp.float32)
        far_embed = far_ref[far, :EMB, :]
        near_vec = jnp.concatenate([near_ref[near, EMB:, :], ones], axis=0)
        far_vec = jnp.concatenate([far_ref[far, EMB:, :], ones], axis=0)
        scores = jnp.concatenate(
            [
                jnp.dot(
                    near_ref[near, :EMB, half * 256 : half * 256 + 256],
                    far_embed,
                    preferred_element_type=jnp.float32,
                )
                for half in range(2)
            ],
            axis=0,
        )
        tile = (0.5 * jnp.tanh(scores) + 0.5).astype(jnp.bfloat16)
        near_terms = lax.dot_general(
            far_vec, tile, (((1,), (1,)), ((), ())), preferred_element_type=jnp.float32
        )
        far_terms = jnp.dot(near_vec, tile, preferred_element_type=jnp.float32)
        return back, near_terms * keep, home, far_terms * mirror

    def each_step(step, carry):
        for copy in fetches(step + AHEAD):
            copy.start()
        for copy in fetches(step):
            copy.wait()
        for back, near_terms, home, far_terms in [one_tile(step, lane) for lane in range(PAIR)]:
            near_sum[back] += near_terms
            far_sum[home] += far_terms
        return carry

    steps = lax.div(found + PAIR - 1, PAIR)
    lax.fori_loop(0, steps, each_step, 0)
    for late in range(AHEAD):
        for copy in fetches(steps + late):
            copy.wait()
    near_keep[...] = near_sum[: Z // 2]
    near_give[...] = near_sum[Z // 2 :].astype(jnp.bfloat16)
    far_keep[...] = far_sum[: X * Y]
    far_give[...] = far_sum[X * Y :].astype(jnp.bfloat16)


def finish_kernel(gram_ref, walked_ref, basis_out, factor_out, wide_ref):
    row = lax.broadcasted_iota(jnp.int32, (VEC, 128), 0)
    lane = lax.broadcasted_iota(jnp.int32, (VEC, 128), 1)
    wide_ref[...] = (lane == row + VEC).astype(jnp.float32)
    wide_ref[:, :VEC] = gram_ref[...]
    wide = wide_ref[...]
    factor = jnp.zeros((VEC, 128), jnp.float32)
    for step in range(VEC):
        pivot = wide[step : step + 1, step : step + 1]
        root = lax.rsqrt(pivot)
        root = root * (1.5 - 0.5 * pivot * root * root)
        scaled = wide[step : step + 1, :] * root
        column = jnp.broadcast_to(wide[:, step : step + 1] * root, (VEC, 128))
        factor = jnp.where((lane == step) & (row >= step), column, factor)
        lower = jnp.where(row > step, wide - column * scaled, wide)
        wide = jnp.where(row == step, jnp.broadcast_to(scaled, (VEC, 128)), lower)
    wide_ref[...] = wide
    basis_out[...] = jnp.dot(
        wide_ref[:, VEC : 2 * VEC],
        walked_ref[...],
        precision=lax.Precision.HIGHEST,
        preferred_element_type=jnp.float32,
    )
    factor_out[...] = factor[:, :VEC]


def shift(values, axis, size, by):
    return lax.ppermute(values, axis, [(i, (i + by) % size) for i in range(size)])


def swap(values, axis, size, bit):
    return lax.ppermute(values, axis, [(i, i ^ bit) for i in range(size)])


def on_device(embeddings, vectors, block_pairs, counts):
    score_scale = 0.5 / math.sqrt(EMB)
    vector_bf16 = vectors.astype(jnp.bfloat16)
    far_send = lax.optimization_barrier(jnp.concatenate([embeddings, vector_bf16], axis=0))
    far_all = lax.all_gather(far_send, FAR)
    turned = embeddings.T
    near_send = jnp.concatenate(
        [
            jnp.concatenate([turned[:256], turned[256:]], axis=1)
            * jnp.asarray(score_scale, jnp.bfloat16),
            vector_bf16,
        ],
        axis=0,
    )
    ring = {0: near_send}
    for step in range(1, Z // 2 + 1):
        ring[Z - step] = shift(ring[(Z - step + 1) % Z], "z", Z, 1)
        if step < Z // 2:
            ring[step] = shift(ring[step - 1], "z", Z, -1)
    near_blocks = [ring[i] for i in range(Z)]
    own_list = jnp.concatenate(
        [block_pairs.reshape(-1), counts, jnp.zeros((128 - 2 * MAXP - 1,), jnp.int32)]
    )
    lists = jnp.stack([own_list] + [shift(own_list, "y", Y, by) for by in (1, 2, 3)])
    place = jnp.stack([lax.axis_index(name) for name in ("y", "k", "z")]).astype(jnp.int32)
    smem = pl.BlockSpec(memory_space=pltpu.SMEM)
    vmem = pl.BlockSpec(memory_space=pltpu.VMEM)
    picked = pl.pallas_call(
        select_kernel,
        out_shape=jax.ShapeDtypeStruct((SLOTS,), jnp.int32),
        in_specs=[smem, smem],
        out_specs=smem,
        name="select_pairs",
    )(place, lists)
    near_total, near_give, far_total, far_give = pl.pallas_call(
        tile_kernel,
        out_shape=[
            jax.ShapeDtypeStruct((Z // 2, AUG, BS), jnp.float32),
            jax.ShapeDtypeStruct((Z // 2, AUG, BS), jnp.bfloat16),
            jax.ShapeDtypeStruct((X * Y, AUG, BS), jnp.float32),
            jax.ShapeDtypeStruct((X * Y, AUG, BS), jnp.bfloat16),
        ],
        in_specs=[smem] + [pl.BlockSpec(memory_space=pl.ANY)] * (1 + Z),
        out_specs=[vmem] * 4,
        scratch_shapes=[
            pltpu.VMEM((Z, EMB + VEC, BS), jnp.bfloat16),
            pltpu.VMEM((PAIR * (AHEAD + 1), EMB + VEC, BS), jnp.bfloat16),
            pltpu.VMEM((Z, AUG, BS), jnp.float32),
            pltpu.VMEM((FARS, AUG, BS), jnp.float32),
            pltpu.SemaphoreType.DMA((Z + PAIR * (AHEAD + 1),)),
        ],
        compiler_params=pltpu.CompilerParams(vmem_limit_bytes=48 * 1024 * 1024),
        name="tiles",
    )(picked, far_all, *near_blocks)
    far_taken = swap(far_give, "k", K, 1)
    far_pair = (far_total + far_taken.astype(jnp.float32)).astype(jnp.bfloat16)
    far_back = lax.all_to_all(far_pair, ("x", "y"), 0, 0)
    for bit in (1, 2, 4):
        left = near_total.shape[0] if bit == 1 else near_total.shape[0] // 2
        give = near_give if bit == 1 else near_total[left:].astype(jnp.bfloat16)
        near_total = near_total[:left] + swap(give, "z", Z, bit).astype(jnp.float32)
    total = near_total[0] + jnp.sum(far_back.astype(jnp.float32), axis=0)
    walked = total[:VEC] / total[VEC : VEC + 1]
    points = BS * X * K * Z * Y
    local_gram = jnp.dot(
        walked, walked.T, precision=lax.Precision.HIGHEST, preferred_element_type=jnp.float32
    )
    partial_gram = local_gram.reshape(1, 8, 128)
    for group in (("x", "y"), ("k", "z")):
        shares = lax.all_to_all(jnp.broadcast_to(partial_gram, (16, 8, 128)), group, 0, 0)
        partial_gram = jnp.sum(shares, axis=0, keepdims=True)
    gram_matrix = partial_gram.reshape(VEC, VEC) / points
    embedding_basis, gram_factor = pl.pallas_call(
        finish_kernel,
        out_shape=[
            jax.ShapeDtypeStruct((VEC, BS), jnp.float32),
            jax.ShapeDtypeStruct((VEC, VEC), jnp.float32),
        ],
        in_specs=[vmem, vmem],
        out_specs=[vmem, vmem],
        scratch_shapes=[pltpu.VMEM((VEC, 128), jnp.float32)],
        name="finish",
    )(gram_matrix, walked)
    return (embedding_basis, gram_factor)


def solution(mesh):
    fine = Mesh(mesh.devices.reshape(X, K, Z, Y), EVERY)
    in_specs = (P(None, EVERY), P(None, EVERY), P(EVERY, None), P(EVERY))
    out_specs = (P(None, EVERY), P())
    return jax.shard_map(
        on_device, mesh=fine, in_specs=in_specs, out_specs=out_specs, check_vma=False
    )
```

```python
import functools
import math

import jax
import jax.numpy as jnp
from jax import lax
from jax.experimental import pallas as pl
from jax.experimental.pallas import tpu as pltpu
from jax.sharding import Mesh
from jax.sharding import PartitionSpec as P

X, K, Z, Y = 4, 2, 8, 4
AXIS_Y = ("h", "l")
FAR = ("x", "k", "l")
EVERY = ("x", "k", "z", "h", "l")
FARS = X * K * Y
BS = 512
EMB = 256
VEC = 32
AUG = 48
MAXP = 24
SLOTS = 128
PAIR = 2
AHEAD = 2


def select_kernel(place_ref, lists_ref, picked_ref):
    own_y = place_ref[0]
    own_k = place_ref[1]
    own_z = place_ref[2]

    def each_list(which, found):
        def each_slot(slot, found):
            row_block = lists_ref[which, 2 * slot]
            col_block = lists_ref[which, 2 * slot + 1]
            row_z = (row_block >> 2) & 7
            near = (row_z - own_z) & 7
            apart = row_z ^ own_z
            back = (apart & 1) * 4 + (apart & 2) + (apart >> 2)
            col_row = col_block >> 5
            col_y = col_block & 3
            far = col_row * Y + (col_y & 1) * 2 + ((col_y >> 1) ^ (own_y >> 1))
            home = ((col_row & 1) ^ own_k) * (X * Y) + (col_row >> 1) * Y + (col_block & 3)
            same = (row_block == col_block).astype(jnp.int32)
            picked_ref[found + 1] = (((same * 8 + back) * 8 + near) * FARS + home) * FARS + far
            return found + ((row_block & 3) == own_y).astype(jnp.int32)

        return lax.fori_loop(0, lists_ref[which, 2 * MAXP], each_slot, found)

    picked_ref[0] = lax.fori_loop(0, Y, each_list, jnp.int32(0))


def tile_kernel(picked_ref, far_hbm, *refs):
    near_hbm = refs[:Z]
    near_keep, near_give, far_keep, far_give, near_ref, far_ref, near_sum, far_sum, sems = refs[Z:]
    found = picked_ref[0]

    def code_of(number):
        return jnp.where(number < found, picked_ref[number + 1], 0)

    def fetches(step):
        ring = lax.rem(step, AHEAD + 1) * PAIR
        return [
            pltpu.make_async_copy(
                far_hbm.at[code_of(step * PAIR + lane) & 31],
                far_ref.at[ring + lane],
                sems.at[Z + ring + lane],
            )
            for lane in range(PAIR)
        ]

    copies = [
        pltpu.make_async_copy(near_hbm[slot], near_ref.at[slot], sems.at[slot]) for slot in range(Z)
    ]
    for copy in copies:
        copy.start()
    for step in range(AHEAD):
        for copy in fetches(jnp.int32(step)):
            copy.start()
    near_sum[...] = jnp.zeros_like(near_sum)
    far_sum[...] = jnp.zeros_like(far_sum)
    ones = (lax.broadcasted_iota(jnp.int32, (AUG - VEC, BS), 0) == 0).astype(jnp.bfloat16)
    for copy in copies:
        copy.wait()

    def one_tile(step, lane):
        number = step * PAIR + lane
        live = number < found
        code = code_of(number)
        far = lax.rem(step, AHEAD + 1) * PAIR + lane
        home = (code >> 5) & 31
        near = (code >> 10) & 7
        back = (code >> 13) & 7
        keep = jnp.where(live, 1.0, 0.0).astype(jnp.float32)
        mirror = jnp.where(live & ((code >> 16) == 0), 1.0, 0.0).astype(jnp.float32)
        far_embed = far_ref[far, :EMB, :]
        near_vec = jnp.concatenate([near_ref[near, EMB:, :], ones], axis=0)
        far_vec = jnp.concatenate([far_ref[far, EMB:, :], ones], axis=0)
        scores = jnp.concatenate(
            [
                jnp.dot(
                    near_ref[near, :EMB, half * 256 : half * 256 + 256],
                    far_embed,
                    preferred_element_type=jnp.float32,
                )
                for half in range(2)
            ],
            axis=0,
        )
        tile = (0.5 * jnp.tanh(scores) + 0.5).astype(jnp.bfloat16)
        near_terms = lax.dot_general(
            far_vec, tile, (((1,), (1,)), ((), ())), preferred_element_type=jnp.float32
        )
        far_terms = jnp.dot(near_vec, tile, preferred_element_type=jnp.float32)
        return back, near_terms * keep, home, far_terms * mirror

    def each_step(step, carry):
        for copy in fetches(step + AHEAD):
            copy.start()
        for copy in fetches(step):
            copy.wait()
        for back, near_terms, home, far_terms in [one_tile(step, lane) for lane in range(PAIR)]:
            near_sum[back] += near_terms
            far_sum[home] += far_terms
        return carry

    steps = lax.div(found + PAIR - 1, PAIR)
    lax.fori_loop(0, steps, each_step, 0)
    for late in range(AHEAD):
        for copy in fetches(steps + late):
            copy.wait()
    near_keep[...] = near_sum[: Z // 2]
    near_give[...] = near_sum[Z // 2 :].astype(jnp.bfloat16)
    far_keep[...] = far_sum[: X * Y]
    far_give[...] = far_sum[X * Y :].astype(jnp.bfloat16)


def finish_kernel(gram_ref, walked_ref, basis_out, factor_out, wide_ref):
    row = lax.broadcasted_iota(jnp.int32, (VEC, 128), 0)
    lane = lax.broadcasted_iota(jnp.int32, (VEC, 128), 1)
    wide_ref[...] = (lane == row + VEC).astype(jnp.float32)
    wide_ref[:, :VEC] = gram_ref[...]
    wide = wide_ref[...]
    factor = jnp.zeros((VEC, 128), jnp.float32)
    for step in range(VEC):
        pivot = wide[step : step + 1, step : step + 1]
        root = lax.rsqrt(pivot)
        root = root * (1.5 - 0.5 * pivot * root * root)
        scaled = wide[step : step + 1, :] * root
        column = jnp.broadcast_to(wide[:, step : step + 1] * root, (VEC, 128))
        factor = jnp.where((lane == step) & (row >= step), column, factor)
        lower = jnp.where(row > step, wide - column * scaled, wide)
        wide = jnp.where(row == step, jnp.broadcast_to(scaled, (VEC, 128)), lower)
    wide_ref[...] = wide
    basis_out[...] = jnp.dot(
        wide_ref[:, VEC : 2 * VEC],
        walked_ref[...],
        precision=lax.Precision.HIGHEST,
        preferred_element_type=jnp.float32,
    )
    factor_out[...] = factor[:, :VEC]


def shift(values, axis, size, by):
    return lax.ppermute(values, axis, [(i, (i + by) % size) for i in range(size)])


def swap(values, axis, size, bit):
    return lax.ppermute(values, axis, [(i, i ^ bit) for i in range(size)])


def on_device(embeddings, vectors, block_pairs, counts):
    score_scale = 0.5 / math.sqrt(EMB)
    vector_bf16 = vectors.astype(jnp.bfloat16)
    far_send = lax.optimization_barrier(jnp.concatenate([embeddings, vector_bf16], axis=0))
    far_two = jnp.stack([far_send, swap(far_send, "h", 2, 1)])
    far_all = lax.all_gather(far_two, FAR).reshape((FARS,) + far_send.shape)
    turned = embeddings.T
    near_send = jnp.concatenate(
        [
            jnp.concatenate([turned[:256], turned[256:]], axis=1)
            * jnp.asarray(score_scale, jnp.bfloat16),
            vector_bf16,
        ],
        axis=0,
    )
    ring = {0: near_send}
    for step in range(1, Z // 2 + 1):
        ring[Z - step] = shift(ring[(Z - step + 1) % Z], "z", Z, 1)
        if step < Z // 2:
            ring[step] = shift(ring[step - 1], "z", Z, -1)
    near_blocks = [ring[i] for i in range(Z)]
    own_list = jnp.concatenate(
        [block_pairs.reshape(-1), counts, jnp.zeros((128 - 2 * MAXP - 1,), jnp.int32)]
    )
    lists = jnp.stack([own_list] + [shift(own_list, AXIS_Y, Y, by) for by in (1, 2, 3)])
    place = jnp.stack([lax.axis_index(name) for name in (AXIS_Y, "k", "z")]).astype(jnp.int32)
    smem = pl.BlockSpec(memory_space=pltpu.SMEM)
    vmem = pl.BlockSpec(memory_space=pltpu.VMEM)
    picked = pl.pallas_call(
        select_kernel,
        out_shape=jax.ShapeDtypeStruct((SLOTS,), jnp.int32),
        in_specs=[smem, smem],
        out_specs=smem,
        name="select_pairs",
    )(place, lists)
    near_total, near_give, far_total, far_give = pl.pallas_call(
        tile_kernel,
        out_shape=[
            jax.ShapeDtypeStruct((Z // 2, AUG, BS), jnp.float32),
            jax.ShapeDtypeStruct((Z // 2, AUG, BS), jnp.bfloat16),
            jax.ShapeDtypeStruct((X * Y, AUG, BS), jnp.float32),
            jax.ShapeDtypeStruct((X * Y, AUG, BS), jnp.bfloat16),
        ],
        in_specs=[smem] + [pl.BlockSpec(memory_space=pl.ANY)] * (1 + Z),
        out_specs=[vmem] * 4,
        scratch_shapes=[
            pltpu.VMEM((Z, EMB + VEC, BS), jnp.bfloat16),
            pltpu.VMEM((PAIR * (AHEAD + 1), EMB + VEC, BS), jnp.bfloat16),
            pltpu.VMEM((Z, AUG, BS), jnp.float32),
            pltpu.VMEM((FARS, AUG, BS), jnp.float32),
            pltpu.SemaphoreType.DMA((Z + PAIR * (AHEAD + 1),)),
        ],
        compiler_params=pltpu.CompilerParams(vmem_limit_bytes=48 * 1024 * 1024),
        name="tiles",
    )(picked, far_all, *near_blocks)
    far_taken = swap(far_give, "k", K, 1)
    far_pair = (far_total + far_taken.astype(jnp.float32)).astype(jnp.bfloat16)
    far_back = lax.all_to_all(far_pair, ("x",) + AXIS_Y, 0, 0)
    for bit in (1, 2, 4):
        left = near_total.shape[0] if bit == 1 else near_total.shape[0] // 2
        give = near_give if bit == 1 else near_total[left:].astype(jnp.bfloat16)
        near_total = near_total[:left] + swap(give, "z", Z, bit).astype(jnp.float32)
    total = near_total[0] + jnp.sum(far_back.astype(jnp.float32), axis=0)
    walked = total[:VEC] / total[VEC : VEC + 1]
    points = BS * X * K * Z * Y
    local_gram = jnp.dot(
        walked, walked.T, precision=lax.Precision.HIGHEST, preferred_element_type=jnp.float32
    )
    partial_gram = local_gram.reshape(1, 8, 128)
    for group in (("x",) + AXIS_Y, ("k", "z")):
        shares = lax.all_to_all(jnp.broadcast_to(partial_gram, (16, 8, 128)), group, 0, 0)
        partial_gram = jnp.sum(shares, axis=0, keepdims=True)
    gram_matrix = partial_gram.reshape(VEC, VEC) / points
    embedding_basis, gram_factor = pl.pallas_call(
        finish_kernel,
        out_shape=[
            jax.ShapeDtypeStruct((VEC, BS), jnp.float32),
            jax.ShapeDtypeStruct((VEC, VEC), jnp.float32),
        ],
        in_specs=[vmem, vmem],
        out_specs=[vmem, vmem],
        scratch_shapes=[pltpu.VMEM((VEC, 128), jnp.float32)],
        name="finish",
    )(gram_matrix, walked)
    return (embedding_basis, gram_factor)


def solution(mesh):
    fine = Mesh(mesh.devices.reshape(X, K, Z, 2, 2), EVERY)
    in_specs = (P(None, EVERY), P(None, EVERY), P(EVERY, None), P(EVERY))
    out_specs = (P(None, EVERY), P())
    return jax.shard_map(
        on_device, mesh=fine, in_specs=in_specs, out_specs=out_specs, check_vma=False
    )
```

```python
import functools
import math

import jax
import jax.numpy as jnp
from jax import lax
from jax.experimental import pallas as pl
from jax.experimental.pallas import tpu as pltpu
from jax.sharding import Mesh
from jax.sharding import PartitionSpec as P

X, K, Z, Y = 4, 2, 8, 4
FAR = ("x", "k", "y")
EVERY = ("x", "k", "z", "y")
FARS = X * K * Y
BS = 512
EMB = 256
VEC = 32
AUG = 48
SENT = 40
MAXP = 24
SLOTS = 128
PAIR = 4
AHEAD = 1


def select_kernel(place_ref, lists_ref, picked_ref):
    own_y = place_ref[0]
    own_k = place_ref[1]
    own_z = place_ref[2]

    def each_list(which, found):
        def each_slot(slot, found):
            row_block = lists_ref[which, 2 * slot]
            col_block = lists_ref[which, 2 * slot + 1]
            row_z = (row_block >> 2) & 7
            near = (row_z - own_z) & 7
            apart = row_z ^ own_z
            back = (apart & 1) * 4 + (apart & 2) + (apart >> 2)
            col_row = col_block >> 5
            far = col_row * Y + (col_block & 3)
            home = ((col_row & 1) ^ own_k) * (X * Y) + (col_row >> 1) * Y + (col_block & 3)
            same = (row_block == col_block).astype(jnp.int32)
            picked_ref[found + 1] = (((same * 8 + back) * 8 + near) * FARS + home) * FARS + far
            return found + ((row_block & 3) == own_y).astype(jnp.int32)

        return lax.fori_loop(0, lists_ref[which, 2 * MAXP], each_slot, found)

    picked_ref[0] = lax.fori_loop(0, Y, each_list, jnp.int32(0))


def tile_kernel(picked_ref, far_hbm, *refs):
    near_hbm = refs[:Z]
    near_keep, near_give, far_keep, far_give, near_ref, far_ref, near_sum, far_sum, sems = refs[Z:]
    found = picked_ref[0]

    def code_of(number):
        return jnp.where(number < found, picked_ref[number + 1], 0)

    def fetches(step):
        ring = lax.rem(step, AHEAD + 1) * PAIR
        return [
            pltpu.make_async_copy(
                far_hbm.at[code_of(step * PAIR + lane) & 31],
                far_ref.at[ring + lane],
                sems.at[Z + ring + lane],
            )
            for lane in range(PAIR)
        ]

    copies = [
        pltpu.make_async_copy(near_hbm[slot], near_ref.at[slot], sems.at[slot]) for slot in range(Z)
    ]
    for copy in copies:
        copy.start()
    for step in range(AHEAD):
        for copy in fetches(jnp.int32(step)):
            copy.start()
    near_sum[...] = jnp.zeros_like(near_sum)
    far_sum[...] = jnp.zeros_like(far_sum)
    ones = (lax.broadcasted_iota(jnp.int32, (AUG - VEC, BS), 0) == 0).astype(jnp.bfloat16)
    for copy in copies:
        copy.wait()

    def one_tile(step, lane):
        number = step * PAIR + lane
        live = number < found
        code = code_of(number)
        far = lax.rem(step, AHEAD + 1) * PAIR + lane
        home = (code >> 5) & 31
        near = (code >> 10) & 7
        back = (code >> 13) & 7
        keep = jnp.where(live, 1.0, 0.0).astype(jnp.float32)
        mirror = jnp.where(live & ((code >> 16) == 0), 1.0, 0.0).astype(jnp.float32)
        far_embed = far_ref[far, :EMB, :]
        near_vec = jnp.concatenate([near_ref[near, EMB:, :], ones], axis=0)
        far_vec = jnp.concatenate([far_ref[far, EMB:, :], ones], axis=0)
        scores = jnp.concatenate(
            [
                jnp.dot(
                    near_ref[near, :EMB, half * 256 : half * 256 + 256],
                    far_embed,
                    preferred_element_type=jnp.float32,
                )
                for half in range(2)
            ],
            axis=0,
        )
        tile = (0.5 * jnp.tanh(scores) + 0.5).astype(jnp.bfloat16)
        near_terms = lax.dot_general(
            far_vec, tile, (((1,), (1,)), ((), ())), preferred_element_type=jnp.float32
        )
        far_terms = jnp.dot(near_vec, tile, preferred_element_type=jnp.float32)
        return back, near_terms * keep, home, far_terms * mirror

    def each_step(step, carry):
        for copy in fetches(step + AHEAD):
            copy.start()
        for copy in fetches(step):
            copy.wait()
        for back, near_terms, home, far_terms in [one_tile(step, lane) for lane in range(PAIR)]:
            near_sum[back] += near_terms
            far_sum[home] += far_terms
        return carry

    steps = lax.div(found + PAIR - 1, PAIR)
    lax.fori_loop(0, steps, each_step, 0)
    for late in range(AHEAD):
        for copy in fetches(steps + late):
            copy.wait()
    near_keep[...] = near_sum[: Z // 2]
    near_give[...] = near_sum[Z // 2 :].astype(jnp.bfloat16)
    far_keep[...] = far_sum[: X * Y]
    far_give[...] = far_sum[X * Y :].astype(jnp.bfloat16)


def finish_kernel(gram_ref, walked_ref, basis_out, factor_out, wide_ref):
    row = lax.broadcasted_iota(jnp.int32, (VEC, 128), 0)
    lane = lax.broadcasted_iota(jnp.int32, (VEC, 128), 1)
    wide_ref[...] = (lane == row + VEC).astype(jnp.float32)
    wide_ref[:, :VEC] = gram_ref[...]
    wide = wide_ref[...]
    factor = jnp.zeros((VEC, 128), jnp.float32)
    for step in range(VEC):
        pivot = wide[step : step + 1, step : step + 1]
        root = lax.rsqrt(pivot)
        root = root * (1.5 - 0.5 * pivot * root * root)
        scaled = wide[step : step + 1, :] * root
        column = jnp.broadcast_to(wide[:, step : step + 1] * root, (VEC, 128))
        factor = jnp.where((lane == step) & (row >= step), column, factor)
        lower = jnp.where(row > step, wide - column * scaled, wide)
        wide = jnp.where(row == step, jnp.broadcast_to(scaled, (VEC, 128)), lower)
    wide_ref[...] = wide
    basis_out[...] = jnp.dot(
        wide_ref[:, VEC : 2 * VEC],
        walked_ref[...],
        precision=lax.Precision.HIGHEST,
        preferred_element_type=jnp.float32,
    )
    factor_out[...] = factor[:, :VEC]


def shift(values, axis, size, by):
    return lax.ppermute(values, axis, [(i, (i + by) % size) for i in range(size)])


def swap(values, axis, size, bit):
    return lax.ppermute(values, axis, [(i, i ^ bit) for i in range(size)])


def on_device(embeddings, vectors, block_pairs, counts):
    score_scale = 0.5 / math.sqrt(EMB)
    vector_bf16 = vectors.astype(jnp.bfloat16)
    far_send = jnp.concatenate([embeddings, vector_bf16], axis=0)
    far_send, embeddings = lax.optimization_barrier((far_send, embeddings))
    far_all = lax.all_gather(far_send, FAR)
    turned = embeddings.T
    near_send = jnp.concatenate(
        [
            jnp.concatenate([turned[:256], turned[256:]], axis=1)
            * jnp.asarray(score_scale, jnp.bfloat16),
            vector_bf16,
        ],
        axis=0,
    )
    ring = {0: near_send}
    for step in range(1, Z // 2 + 1):
        ring[Z - step] = shift(ring[(Z - step + 1) % Z], "z", Z, 1)
        if step < Z // 2:
            ring[step] = shift(ring[step - 1], "z", Z, -1)
    near_blocks = [ring[i] for i in range(Z)]
    own_list = jnp.concatenate(
        [block_pairs.reshape(-1), counts, jnp.zeros((128 - 2 * MAXP - 1,), jnp.int32)]
    )
    lists = jnp.stack([own_list] + [shift(own_list, "y", Y, by) for by in (1, 2, 3)])
    place = jnp.stack([lax.axis_index(name) for name in ("y", "k", "z")]).astype(jnp.int32)
    smem = pl.BlockSpec(memory_space=pltpu.SMEM)
    vmem = pl.BlockSpec(memory_space=pltpu.VMEM)
    picked = pl.pallas_call(
        select_kernel,
        out_shape=jax.ShapeDtypeStruct((SLOTS,), jnp.int32),
        in_specs=[smem, smem],
        out_specs=smem,
        name="select_pairs",
    )(place, lists)
    near_total, near_give, far_total, far_give = pl.pallas_call(
        tile_kernel,
        out_shape=[
            jax.ShapeDtypeStruct((Z // 2, AUG, BS), jnp.float32),
            jax.ShapeDtypeStruct((Z // 2, AUG, BS), jnp.bfloat16),
            jax.ShapeDtypeStruct((X * Y, AUG, BS), jnp.float32),
            jax.ShapeDtypeStruct((X * Y, AUG, BS), jnp.bfloat16),
        ],
        in_specs=[smem] + [pl.BlockSpec(memory_space=pl.ANY)] * (1 + Z),
        out_specs=[vmem] * 4,
        scratch_shapes=[
            pltpu.VMEM((Z, EMB + VEC, BS), jnp.bfloat16),
            pltpu.VMEM((PAIR * (AHEAD + 1), EMB + VEC, BS), jnp.bfloat16),
            pltpu.VMEM((Z, AUG, BS), jnp.float32),
            pltpu.VMEM((FARS, AUG, BS), jnp.float32),
            pltpu.SemaphoreType.DMA((Z + PAIR * (AHEAD + 1),)),
        ],
        compiler_params=pltpu.CompilerParams(vmem_limit_bytes=48 * 1024 * 1024),
        name="tiles",
    )(picked, far_all, *near_blocks)
    far_taken = swap(far_give, "k", K, 1)
    far_pair = (far_total + far_taken.astype(jnp.float32))[:, :SENT].astype(jnp.bfloat16)
    far_back = lax.all_to_all(far_pair, ("x", "y"), 0, 0)
    for bit in (1, 2, 4):
        left = near_total.shape[0] if bit == 1 else near_total.shape[0] // 2
        give = near_give if bit == 1 else near_total[left:].astype(jnp.bfloat16)
        near_total = (near_total[:left] + swap(give, "z", Z, bit).astype(jnp.float32))[:, :SENT]
    total = near_total[0] + jnp.sum(far_back.astype(jnp.float32), axis=0)
    walked = total[:VEC] / total[VEC : VEC + 1]
    points = BS * X * K * Z * Y
    local_gram = jnp.dot(
        walked, walked.T, precision=lax.Precision.HIGHEST, preferred_element_type=jnp.float32
    )
    partial_gram = local_gram.reshape(1, 8, 128)
    for group in (("x", "y"), ("k", "z")):
        shares = lax.all_to_all(jnp.broadcast_to(partial_gram, (16, 8, 128)), group, 0, 0)
        partial_gram = jnp.sum(shares, axis=0, keepdims=True)
    gram_matrix = partial_gram.reshape(VEC, VEC) / points
    embedding_basis, gram_factor = pl.pallas_call(
        finish_kernel,
        out_shape=[
            jax.ShapeDtypeStruct((VEC, BS), jnp.float32),
            jax.ShapeDtypeStruct((VEC, VEC), jnp.float32),
        ],
        in_specs=[vmem, vmem],
        out_specs=[vmem, vmem],
        scratch_shapes=[pltpu.VMEM((VEC, 128), jnp.float32)],
        name="finish",
    )(gram_matrix, walked)
    return (embedding_basis, gram_factor)


def solution(mesh):
    fine = Mesh(mesh.devices.reshape(X, K, Z, Y), EVERY)
    in_specs = (P(None, EVERY), P(None, EVERY), P(EVERY, None), P(EVERY))
    out_specs = (P(None, EVERY), P())
    return jax.shard_map(
        on_device, mesh=fine, in_specs=in_specs, out_specs=out_specs, check_vma=False
    )
```

```python
import functools
import math

import jax
import jax.numpy as jnp
from jax import lax
from jax.experimental import pallas as pl
from jax.experimental.pallas import tpu as pltpu
from jax.sharding import Mesh
from jax.sharding import PartitionSpec as P

X, K, Z, Y = 4, 2, 8, 4
FAR = ("x", "k", "y")
EVERY = ("x", "k", "z", "y")
FARS = X * K * Y
BS = 512
EMB = 256
VEC = 32
AUG = 48
SENT = 40
MAXP = 24
SLOTS = 128
PAIR = 4
AHEAD = 1


def select_kernel(place_ref, lists_ref, picked_ref):
    own_y = place_ref[0]
    own_k = place_ref[1]
    own_z = place_ref[2]

    def each_list(which, found):
        def each_slot(slot, found):
            row_block = lists_ref[which, 2 * slot]
            col_block = lists_ref[which, 2 * slot + 1]
            row_z = (row_block >> 2) & 7
            near = (row_z - own_z) & 7
            apart = row_z ^ own_z
            back = (apart & 1) * 4 + (apart & 2) + (apart >> 2)
            col_row = col_block >> 5
            far = col_row * Y + (col_block & 3)
            home = ((col_row & 1) ^ own_k) * (X * Y) + (col_row >> 1) * Y + (col_block & 3)
            same = (row_block == col_block).astype(jnp.int32)
            picked_ref[found + 1] = (((same * 8 + back) * 8 + near) * FARS + home) * FARS + far
            return found + ((row_block & 3) == own_y).astype(jnp.int32)

        return lax.fori_loop(0, lists_ref[which, 2 * MAXP], each_slot, found)

    picked_ref[0] = lax.fori_loop(0, Y, each_list, jnp.int32(0))


def tile_kernel(picked_ref, far_hbm, *refs):
    near_hbm = refs[:Z]
    near_keep, near_give, far_keep, far_give, near_ref, far_ref, near_sum, far_sum, sems = refs[Z:]
    found = picked_ref[0]

    def code_of(number):
        return jnp.where(number < found, picked_ref[number + 1], 0)

    def fetches(step):
        ring = lax.rem(step, AHEAD + 1) * PAIR
        return [
            pltpu.make_async_copy(
                far_hbm.at[code_of(step * PAIR + lane) & 31],
                far_ref.at[ring + lane],
                sems.at[Z + ring + lane],
            )
            for lane in range(PAIR)
        ]

    copies = [
        pltpu.make_async_copy(near_hbm[slot], near_ref.at[slot], sems.at[slot]) for slot in range(Z)
    ]
    for copy in copies:
        copy.start()
    for step in range(AHEAD):
        for copy in fetches(jnp.int32(step)):
            copy.start()
    near_sum[...] = jnp.zeros_like(near_sum)
    far_sum[...] = jnp.zeros_like(far_sum)
    ones = (lax.broadcasted_iota(jnp.int32, (AUG - VEC, BS), 0) == 0).astype(jnp.bfloat16)
    for copy in copies:
        copy.wait()

    def one_tile(step, lane):
        number = step * PAIR + lane
        live = number < found
        code = code_of(number)
        far = lax.rem(step, AHEAD + 1) * PAIR + lane
        home = (code >> 5) & 31
        near = (code >> 10) & 7
        back = (code >> 13) & 7
        keep = jnp.where(live, 1.0, 0.0).astype(jnp.float32)
        mirror = jnp.where(live & ((code >> 16) == 0), 1.0, 0.0).astype(jnp.float32)
        far_embed = far_ref[far, :EMB, :]
        near_vec = jnp.concatenate([near_ref[near, EMB:, :], ones], axis=0)
        far_vec = jnp.concatenate([far_ref[far, EMB:, :], ones], axis=0)
        scores = jnp.concatenate(
            [
                jnp.dot(
                    near_ref[near, :EMB, half * 256 : half * 256 + 256],
                    far_embed,
                    preferred_element_type=jnp.float32,
                )
                for half in range(2)
            ],
            axis=0,
        )
        tile = (0.5 * jnp.tanh(scores) + 0.5).astype(jnp.bfloat16)
        near_terms = lax.dot_general(
            far_vec, tile, (((1,), (1,)), ((), ())), preferred_element_type=jnp.float32
        )
        far_terms = jnp.dot(near_vec, tile, preferred_element_type=jnp.float32)
        return back, near_terms * keep, home, far_terms * mirror

    def each_step(step, carry):
        for copy in fetches(step + AHEAD):
            copy.start()
        for copy in fetches(step):
            copy.wait()
        for back, near_terms, home, far_terms in [one_tile(step, lane) for lane in range(PAIR)]:
            near_sum[back] += near_terms
            far_sum[home] += far_terms
        return carry

    steps = lax.div(found + PAIR - 1, PAIR)
    lax.fori_loop(0, steps, each_step, 0)
    for late in range(AHEAD):
        for copy in fetches(steps + late):
            copy.wait()
    near_keep[...] = near_sum[: Z // 2]
    near_give[...] = near_sum[Z // 2 :].astype(jnp.bfloat16)
    far_keep[...] = far_sum[: X * Y]
    far_give[...] = far_sum[X * Y :].astype(jnp.bfloat16)


def finish_kernel(gram_ref, walked_ref, basis_out, factor_out, wide_ref):
    row = lax.broadcasted_iota(jnp.int32, (VEC, 128), 0)
    lane = lax.broadcasted_iota(jnp.int32, (VEC, 128), 1)
    wide_ref[...] = (lane == row + VEC).astype(jnp.float32)
    wide_ref[:, :VEC] = gram_ref[...]
    wide = wide_ref[...]
    factor = jnp.zeros((VEC, 128), jnp.float32)
    for step in range(VEC):
        pivot = wide[step : step + 1, step : step + 1]
        root = lax.rsqrt(pivot)
        root = root * (1.5 - 0.5 * pivot * root * root)
        scaled = wide[step : step + 1, :] * root
        column = jnp.broadcast_to(wide[:, step : step + 1] * root, (VEC, 128))
        factor = jnp.where((lane == step) & (row >= step), column, factor)
        lower = jnp.where(row > step, wide - column * scaled, wide)
        wide = jnp.where(row == step, jnp.broadcast_to(scaled, (VEC, 128)), lower)
    wide_ref[...] = wide
    basis_out[...] = jnp.dot(
        wide_ref[:, VEC : 2 * VEC],
        walked_ref[...],
        precision=lax.Precision.HIGHEST,
        preferred_element_type=jnp.float32,
    )
    factor_out[...] = factor[:, :VEC]


def shift(values, axis, size, by):
    return lax.ppermute(values, axis, [(i, (i + by) % size) for i in range(size)])


def swap(values, axis, size, bit):
    return lax.ppermute(values, axis, [(i, i ^ bit) for i in range(size)])


def on_device(embeddings, vectors, block_pairs, counts):
    score_scale = 0.5 / math.sqrt(EMB)
    vector_bf16 = vectors.astype(jnp.bfloat16)
    far_send = jnp.concatenate([embeddings, vector_bf16], axis=0)
    far_send, embeddings = lax.optimization_barrier((far_send, embeddings))
    far_all = lax.all_gather(far_send, FAR)
    turned = embeddings.T
    near_send = jnp.concatenate(
        [
            jnp.concatenate([turned[:256], turned[256:]], axis=1)
            * jnp.asarray(score_scale, jnp.bfloat16),
            vector_bf16,
        ],
        axis=0,
    )
    ring = {0: near_send}
    for step in range(1, Z // 2 + 1):
        ring[Z - step] = shift(ring[(Z - step + 1) % Z], "z", Z, 1)
        if step < Z // 2:
            ring[step] = shift(ring[step - 1], "z", Z, -1)
    near_blocks = [ring[i] for i in range(Z)]
    own_list = jnp.concatenate(
        [block_pairs.reshape(-1), counts, jnp.zeros((128 - 2 * MAXP - 1,), jnp.int32)]
    )
    lists = jnp.stack([own_list] + [shift(own_list, "y", Y, by) for by in (1, 2, 3)])
    place = jnp.stack([lax.axis_index(name) for name in ("y", "k", "z")]).astype(jnp.int32)
    smem = pl.BlockSpec(memory_space=pltpu.SMEM)
    vmem = pl.BlockSpec(memory_space=pltpu.VMEM)
    picked = pl.pallas_call(
        select_kernel,
        out_shape=jax.ShapeDtypeStruct((SLOTS,), jnp.int32),
        in_specs=[smem, smem],
        out_specs=smem,
        name="select_pairs",
    )(place, lists)
    near_total, near_give, far_total, far_give = pl.pallas_call(
        tile_kernel,
        out_shape=[
            jax.ShapeDtypeStruct((Z // 2, AUG, BS), jnp.float32),
            jax.ShapeDtypeStruct((Z // 2, AUG, BS), jnp.bfloat16),
            jax.ShapeDtypeStruct((X * Y, AUG, BS), jnp.float32),
            jax.ShapeDtypeStruct((X * Y, AUG, BS), jnp.bfloat16),
        ],
        in_specs=[smem] + [pl.BlockSpec(memory_space=pl.ANY)] * (1 + Z),
        out_specs=[vmem] * 4,
        scratch_shapes=[
            pltpu.VMEM((Z, EMB + VEC, BS), jnp.bfloat16),
            pltpu.VMEM((PAIR * (AHEAD + 1), EMB + VEC, BS), jnp.bfloat16),
            pltpu.VMEM((Z, AUG, BS), jnp.float32),
            pltpu.VMEM((FARS, AUG, BS), jnp.float32),
            pltpu.SemaphoreType.DMA((Z + PAIR * (AHEAD + 1),)),
        ],
        compiler_params=pltpu.CompilerParams(vmem_limit_bytes=48 * 1024 * 1024),
        name="tiles",
    )(picked, far_all, *near_blocks)
    far_taken = swap(far_give, "k", K, 1)
    far_pair = (far_total + far_taken.astype(jnp.float32))[:, :SENT].astype(jnp.bfloat16)
    far_back = lax.all_to_all(far_pair, ("x", "y"), 0, 0)
    for bit in (1, 2, 4):
        left = near_total.shape[0] if bit == 1 else near_total.shape[0] // 2
        give = near_give if bit == 1 else near_total[left:].astype(jnp.bfloat16)
        near_total = (near_total[:left] + swap(give, "z", Z, bit).astype(jnp.float32))[:, :SENT]
    total = near_total[0] + jnp.sum(far_back.astype(jnp.float32), axis=0)
    walked = total[:VEC] / total[VEC : VEC + 1]
    points = BS * X * K * Z * Y
    local_gram = jnp.dot(
        walked, walked.T, precision=lax.Precision.HIGHEST, preferred_element_type=jnp.float32
    )
    partial_gram = local_gram.reshape(1, 8, 128)
    for group, ways in ((("x", "k"), X * K), (("z", "y"), Z * Y)):
        shares = lax.all_to_all(jnp.broadcast_to(partial_gram, (ways, 8, 128)), group, 0, 0)
        partial_gram = jnp.sum(shares, axis=0, keepdims=True)
    gram_matrix = partial_gram.reshape(VEC, VEC) / points
    embedding_basis, gram_factor = pl.pallas_call(
        finish_kernel,
        out_shape=[
            jax.ShapeDtypeStruct((VEC, BS), jnp.float32),
            jax.ShapeDtypeStruct((VEC, VEC), jnp.float32),
        ],
        in_specs=[vmem, vmem],
        out_specs=[vmem, vmem],
        scratch_shapes=[pltpu.VMEM((VEC, 128), jnp.float32)],
        name="finish",
    )(gram_matrix, walked)
    return (embedding_basis, gram_factor)


def solution(mesh):
    fine = Mesh(mesh.devices.reshape(X, K, Z, Y), EVERY)
    in_specs = (P(None, EVERY), P(None, EVERY), P(EVERY, None), P(EVERY))
    out_specs = (P(None, EVERY), P())
    return jax.shard_map(
        on_device, mesh=fine, in_specs=in_specs, out_specs=out_specs, check_vma=False
    )
```
